32 devices in a mesh: groups: 2 (over y), seq: 16 (over z, x, core).
Axes of the slice: x: 2, y: 2, z: 4, core: 2. Of those that a mesh axis runs over, the one named last changes fastest.
Arguments:
- grad_rows: bfloat16 [8192, 3584], P(('groups', 'seq')), parts along dimension 0, may hold values from -6 to 6
- route_ids: int32 [8192, 1], P(('groups', 'seq')), parts along dimension 0, may hold values from 0 to 31; in each aligned block of 256 rows (0 to 255, 256 to 511, ...) at most 16 rows name the same one
- audio_proj: bfloat16 [1280, 3584], P(None, 'seq'), may hold values from -0.15625 to 0.15625
- vision_proj: bfloat16 [1280, 3584], P(None, 'seq'), may hold values from -0.15625 to 0.15625
- audio_states: bfloat16 [8192, 1280], P(('groups', 'seq')), parts along dimension 0, may hold values from -120 to 120
- vision_states: bfloat16 [8192, 1280], P(('groups', 'seq')), parts along dimension 0, may hold values from -120 to 120
- audio_gain: float32 [1280], replicated, may hold values from 0.25 to 1.75
- vision_gain: float32 [1280], replicated, may hold values from 0.25 to 1.75
Outputs:
- audio_input_grad: bfloat16 [8192, 1280], P(('groups', 'seq')), parts along dimension 0
- vision_input_grad: bfloat16 [8192, 1280], P(('groups', 'seq')), parts along dimension 0
- gain_grads: float32 [4, 1280], P('groups'), parts along dimension 0
The draws below stay inside these ranges and needn't reach their ends.
There are 2 independent parts, one for each index of `groups`. The reference program is written for one: setup_inputs(seed, part) draws one part's arguments, and reference() takes and returns one part's arrays. A program takes and returns all parts, laid end to end along the dimension named above; an argument that names none is the same for every part. Nothing has to cross between parts.
Inputs may be any that keep to these rules, and one draw needn't show every extreme that they name: `route_ids`: within the rows of one device no number is named by more than 16 rows, a bound that some block reaches; every number is named somewhere.
All inputs are finite; a program needn't handle non-finite values.
Results may differ from the reference program's by a relative error of at most 0.0085.
Values may be sent and summed in bfloat16 or wider, within the bound.
No kernel may reach another device: no remote copies, remote signals or barrier semaphores. Data moves between devices by JAX's collectives and lax.ppermute only.
A program may use at most 128 MiB of HBM per device.

```python
import math
import jax
import jax.numpy as jnp
import numpy as np
from jax import lax

D_LLM = 3584
D_ENC = 1280
ROWS_DEV = 256
CAP = 16
TOKENS = 4096
N_SEQ = 16


def normal_rows(key):
    rough = jnp.clip(jax.random.normal(jax.random.fold_in(key, 1), (TOKENS, D_ENC)), -5.0, 5.0)
    rows = jnp.exp(jax.random.uniform(jax.random.fold_in(key, 2), (TOKENS, 1), minval=0.0, maxval=math.log(10.0)))
    columns = jnp.exp(jax.random.uniform(jax.random.fold_in(key, 3), (1, D_ENC), minval=0.0, maxval=math.log(4.0)))
    return (rough * columns * 0.5 * rows).astype(jnp.bfloat16)


def draw_audio_states(key, part):
    key = jax.random.fold_in(key, 11)
    return normal_rows(key)


def draw_vision_states(key, part):
    key = jax.random.fold_in(key, 23)
    return normal_rows(key)


def level_of(key, dims, pieces, least, top_value):
    level = 1.0
    for dim, blocks in pieces:
        draws = jax.random.uniform(jax.random.fold_in(jax.random.fold_in(key, 6), dim), (blocks,), jnp.float32, least / len(pieces), top_value / len(pieces))
        level = level * jnp.repeat(jnp.exp(draws), dims[dim] // blocks).reshape((-1,) + (1,) * (len(dims) - 1 - dim))
    return level


def assign_block(own_key, own, number, rows, number_of, top, reach, slope):
    ranking = jax.random.permutation(own_key, number_of)
    packed, usual = load_shares(number_of, rows * top, reach, slope, True), load_shares(number_of, rows * top, reach, slope, False)
    places = jnp.arange(number_of)

    def named(tallies, turn):
        used = int((tallies > 0).sum())
        fixed = max(1, used // 4)
        moved = fixed + (places - fixed + turn * (used - fixed)) % max(1, number_of - fixed)
        return jnp.zeros((number_of,), jnp.int32).at[ranking[jnp.where(places < fixed, places, moved)]].set(jnp.asarray(tallies, jnp.int32))

    tallies = jnp.where(number % 4 == 0, named(packed, number // 4), named(usual, number - number // 4 - 1))
    mixed = jax.random.permutation(jax.random.fold_in(own, 3), number_of)
    giver, taker = mixed[0:number_of // 2 * 2:2], mixed[1:number_of // 2 * 2:2]
    margin = jnp.minimum(tallies[giver] - 1, reach - tallies[taker]) // 2
    margin = jnp.where((giver == ranking[0]) | (taker == ranking[0]) | (tallies[taker] == 0), 0, jnp.maximum(margin, 0))
    moved = jax.random.randint(jax.random.fold_in(own, 4), (number_of // 2,), 0, 1 << 20) % (margin + 1)
    tallies = tallies.at[giver].add(-moved).at[taker].add(moved)
    labels = jnp.searchsorted(jnp.cumsum(tallies), jnp.arange(rows * top), side="right").astype(jnp.int32)
    table = labels.reshape(top, rows).T
    table = table[jax.random.permutation(jax.random.fold_in(own, 1), rows)]
    turn = jax.random.randint(jax.random.fold_in(own, 2), (rows, 1), 0, top)
    return jnp.take_along_axis(table, (jnp.arange(top)[None, :] + turn) % top, axis=1)


def load_shares(count, total, bound, lean, full):
    loads = [(1 << 20) // math.isqrt(rank ** lean) + 1 for rank in range(1, count + 1)]
    largest = bound if full else min(bound, max(-(-total // count), total * loads[0] // sum(loads)))
    least = 1 if total - largest >= count - 1 else 0
    holding, surplus = [largest] + [least] * (count - 1), total - largest - least * (count - 1)
    while surplus > 0:
        free = [i for i in range(1, count) if holding[i] < largest] or [i for i in range(1, count) if holding[i] < bound]
        pool, budget = sum([loads[i] for i in free]), surplus
        for i in free:
            addition = min(bound - holding[i], max(1, budget * loads[i] // pool), surplus)
            holding[i] = holding[i] + addition
            surplus = surplus - addition
    return np.array(holding)


def normal_values(own_key, shape, deviation, most, shards=(), kind=jnp.bfloat16):
    values = jax.random.normal(own_key, shape, jnp.float32) * deviation
    if len(shards) > 0:
        values = level_of(own_key, shape, shards, -0.22, 0.18) * values
    return jnp.clip(values, min=-most, max=most).astype(kind)


def setup_inputs(seed: int = 0, part: int = 0) -> dict:
    splits = jax.random.split(jax.random.key(seed), 9)
    part_keys = jax.random.split(jax.random.fold_in(splits[8], part), 9)
    grad_rows = normal_values(part_keys[0], (TOKENS, D_LLM), 1.0, 6.0, ((0, 16),))
    route_ids_keys = jax.random.split(jax.random.fold_in(part_keys[1], 1), TOKENS // ROWS_DEV)
    route_ids_turns = jax.random.permutation(jax.random.fold_in(part_keys[1], 3), TOKENS // ROWS_DEV)
    route_ids = jax.vmap(lambda own, number: assign_block(jax.random.fold_in(part_keys[1], 2), own, number, ROWS_DEV, 2 * N_SEQ, 1, CAP, 2))(route_ids_keys, route_ids_turns).reshape((TOKENS, 1))
    audio_proj = normal_values(splits[2], (D_ENC, D_LLM), D_ENC ** -0.5, 0.15625, ((1, 16),))
    vision_proj = normal_values(splits[3], (D_ENC, D_LLM), D_ENC ** -0.5, 0.15625, ((1, 16),))
    audio_states = draw_audio_states(jax.random.fold_in(jax.random.fold_in(splits[8], part), 71), part)
    vision_states = draw_vision_states(jax.random.fold_in(jax.random.fold_in(splits[8], part), 71), part)
    audio_gain = jnp.clip(1.0 + 0.15 * jax.random.normal(splits[6], (D_ENC,), jnp.float32), 0.25, 1.75)
    vision_gain = jnp.clip(1.0 + 0.15 * jax.random.normal(splits[7], (D_ENC,), jnp.float32), 0.25, 1.75)
    return dict(grad_rows=grad_rows, route_ids=route_ids, audio_proj=audio_proj, vision_proj=vision_proj, audio_states=audio_states, vision_states=vision_states, audio_gain=audio_gain, vision_gain=vision_gain)


def layer_back(states, upstream, gain):
    h = states.astype(jnp.float32)
    mu = lax.optimization_barrier(jnp.mean(h, axis=-1, keepdims=True))
    centred = h - mu
    scale = lax.rsqrt(lax.optimization_barrier(jnp.mean(centred * centred, axis=-1, keepdims=True)) + 1e-05)
    normed = centred * scale
    upper = upstream.astype(jnp.float32)
    scaled = upper * gain[None, :]
    back = scale * (scaled - lax.optimization_barrier(jnp.mean(scaled, axis=-1, keepdims=True)) - normed * lax.optimization_barrier(jnp.mean(scaled * normed, axis=-1, keepdims=True)))
    return (back.astype(jnp.bfloat16), lax.optimization_barrier(jnp.sum(upper * normed, axis=0)))

def rms_back(states, upstream, gain):
    h = states.astype(jnp.float32)
    scale = lax.rsqrt(lax.optimization_barrier(jnp.mean(h * h, axis=-1, keepdims=True)) + 1e-06)
    normed = h * scale
    upper = upstream.astype(jnp.float32)
    scaled = upper * gain[None, :]
    back = scale * (scaled - normed * lax.optimization_barrier(jnp.mean(scaled * normed, axis=-1, keepdims=True)))
    return (back.astype(jnp.bfloat16), lax.optimization_barrier(jnp.sum(upper * normed, axis=0)))

def reference(grad_rows, route_ids, audio_proj, vision_proj, audio_states, vision_states, audio_gain, vision_gain):
    cap = ROWS_DEV // N_SEQ
    kinds = 2 * N_SEQ
    ids = route_ids[:, 0].reshape(N_SEQ, ROWS_DEV)
    onehot = (ids[:, :, None] == jnp.arange(kinds, dtype=jnp.int32)[None, None, :]).astype(jnp.int32)
    earlier = jnp.cumsum(onehot, axis=1) - onehot
    slot = lax.optimization_barrier(jnp.sum(earlier * onehot, axis=2)).astype(jnp.int32)
    source = jnp.arange(N_SEQ, dtype=jnp.int32)[:, None]
    device = ids % N_SEQ
    index = (device * ROWS_DEV + source * cap + slot).reshape(-1).astype(jnp.int32)
    is_audio = (ids // N_SEQ == 0).reshape(-1)
    total = ROWS_DEV * N_SEQ
    outside = jnp.full_like(index, total)
    audio_back = jnp.dot(grad_rows, audio_proj.T, preferred_element_type=jnp.float32).astype(jnp.bfloat16)
    vision_back = jnp.dot(grad_rows, vision_proj.T, preferred_element_type=jnp.float32).astype(jnp.bfloat16)
    upstream_a = jnp.zeros((total, D_ENC), jnp.bfloat16).at[jnp.where(is_audio, index, outside)].set(audio_back, mode='drop')
    upstream_v = jnp.zeros((total, D_ENC), jnp.bfloat16).at[jnp.where(is_audio, outside, index)].set(vision_back, mode='drop')
    audio_grad, audio_part = layer_back(audio_states, upstream_a, audio_gain)
    vision_grad, vision_part = rms_back(vision_states, upstream_v, vision_gain)
    return (audio_grad, vision_grad, jnp.stack([audio_part, vision_part]))
```

```python
import functools

import jax
import jax.numpy as jnp
from jax import lax
from jax.experimental import pallas as pl
from jax.experimental.pallas import tpu as pltpu
from jax.sharding import PartitionSpec as P

F32 = jnp.float32
BF16 = jnp.bfloat16
BOTH = ("groups", "seq")
BIG = 48 * 1024 * 1024
VM = pl.BlockSpec(memory_space=pltpu.VMEM)
SM = pl.BlockSpec(memory_space=pltpu.SMEM)
ANY = pl.BlockSpec(memory_space=pl.ANY)


def place(line, pair, core):
    return (line * 2 + pair) * 2 + core


def flip(value, bit, devices):
    return lax.ppermute(value, "seq", [(i, i ^ bit) for i in range(devices)])


def along(value, moves):
    pairs = []
    for a, b in moves:
        for p in range(2):
            for c in range(2):
                pairs.append((place(a, p, c), place(b, p, c)))
    return lax.ppermute(value, "seq", pairs)


def across(value, lines, devices):
    pairs = []
    for a in lines:
        for p in range(2):
            for c in range(2):
                i = place(a, p, c)
                pairs += [(i, devices + i), (devices + i, i)]
    return lax.ppermute(value, BOTH, pairs)


def multiply(blocks, mine_w, other_w, masks, keep_ref, send_ref):
    rows = blocks[0].shape[0]
    for i, (ref, start) in enumerate(blocks_of(blocks)):
        lhs = ref[start : start + rows, :]
        one = jnp.dot(lhs, mine_w[...], preferred_element_type=F32)
        two = jnp.dot(lhs, other_w[...], preferred_element_type=F32)
        value = jnp.where(masks[i * rows : (i + 1) * rows, :] > 0, one, two)
        half = (i // 2) * rows
        if i % 2 == 0:
            keep_ref[half : half + rows, :] = value
        else:
            send_ref[half : half + rows, :] = value.astype(BF16)


def blocks_of(blocks):
    own, pair, far = blocks
    return [(own, 0), (pair, 0), (far, 0), (far, own.shape[0])]


def product_line(*refs):
    line, masks, own, pair, far = refs[:5]
    parts = refs[5:17]
    keep_ref, send_ref, mine_w, other_w, sems = refs[17:]
    deep = parts[0].shape[0]
    choice = {0: (0, 2, 4, 5), 1: (1, 0, 2, 3), 2: (3, 1, 0, 2), 3: (5, 4, 1, 0)}
    for where, order in choice.items():

        @pl.when(line[0] == where)
        def _():
            for s, k in enumerate(order):
                rows = pl.ds(s * deep, deep)
                pltpu.make_async_copy(parts[k], mine_w.at[rows], sems.at[s]).start()
                pltpu.make_async_copy(parts[6 + k], other_w.at[rows], sems.at[4 + s]).start()

    for s in range(4):
        rows = pl.ds(s * deep, deep)
        pltpu.make_async_copy(parts[0], mine_w.at[rows], sems.at[s]).wait()
        pltpu.make_async_copy(parts[6], other_w.at[rows], sems.at[4 + s]).wait()
    multiply((own, pair, far), mine_w, other_w, masks, keep_ref, send_ref)


def product_plain(masks, own, pair, far, mine_w, other_w, keep_ref, send_ref):
    multiply((own, pair, far), mine_w, other_w, masks, keep_ref, send_ref)


def pack(base_col, base_row, keep, recv, out):
    total = keep.shape[0]
    first = lax.broadcasted_iota(jnp.int32, (total, total), 0)
    second = lax.broadcasted_iota(jnp.int32, (total, total), 1)
    same = jnp.logical_and(base_col[...] == base_row[...], first < second)
    count = jnp.sum(same.astype(F32), axis=0, keepdims=True).astype(jnp.int32)
    slot = base_row[...] + count
    up = (keep[...] + recv[...].astype(F32)).astype(BF16)
    step = out.shape[0] // 2
    for i in range(2):
        place_of = lax.broadcasted_iota(jnp.int32, (step, total), 0) + i * step
        pick = (place_of == slot).astype(F32).astype(BF16)
        out[i * step : (i + 1) * step, :] = jnp.dot(pick, up, preferred_element_type=F32).astype(BF16)


def norms(recv, a_states, v_states, a_gain, v_gain, a_out, v_out, gains):
    rows, width = a_states.shape
    half = width // 2
    inv = 1.0 / width

    def upstream(h, m):
        return recv[:, h, :, m].reshape(rows, half).astype(F32)

    def cols(h):
        return slice(h * half, (h + 1) * half)

    h = a_states[...].astype(F32)
    mu = jnp.sum(h, axis=1, keepdims=True) * inv
    centred = h - mu
    scale = lax.rsqrt(jnp.sum(centred * centred, axis=1, keepdims=True) * inv + 1e-5)
    normed = centred * scale
    ps, pn, parts = 0.0, 0.0, []
    for k in range(2):
        u = upstream(k, 0)
        n = normed[:, cols(k)]
        p = u * a_gain[:, cols(k)]
        ps = ps + jnp.sum(p, axis=1, keepdims=True)
        pn = pn + jnp.sum(p * n, axis=1, keepdims=True)
        gains[0:1, cols(k)] = jnp.sum(u * n, axis=0, keepdims=True)
        parts.append((p, n))
    for k in range(2):
        p, n = parts[k]
        a_out[:, cols(k)] = (scale * (p - ps * inv - n * (pn * inv))).astype(BF16)

    h = v_states[...].astype(F32)
    scale = lax.rsqrt(jnp.sum(h * h, axis=1, keepdims=True) * inv + 1e-6)
    normed = h * scale
    pn, parts = 0.0, []
    for k in range(2):
        u = upstream(k, 1)
        n = normed[:, cols(k)]
        p = u * v_gain[:, cols(k)]
        pn = pn + jnp.sum(p * n, axis=1, keepdims=True)
        gains[1:2, cols(k)] = jnp.sum(u * n, axis=0, keepdims=True)
        parts.append((p, n))
    for k in range(2):
        p, n = parts[k]
        v_out[:, cols(k)] = (scale * (p - n * (pn * inv))).astype(BF16)


def call(body, outs, specs, scratch=()):
    return pl.pallas_call(
        body,
        out_shape=outs,
        in_specs=specs,
        out_specs=jax.tree.map(lambda _: VM, outs),
        scratch_shapes=list(scratch),
        compiler_params=pltpu.CompilerParams(vmem_limit_bytes=BIG),
    )


def on_device(
    grad_rows,
    route_ids,
    audio_proj,
    vision_proj,
    audio_states,
    vision_states,
    audio_gain,
    vision_gain,
):
    devices = lax.axis_size("seq")
    lines = devices // 4
    rows, width = grad_rows.shape
    enc, k = audio_proj.shape
    half = enc // 2
    cap = rows // devices
    group = lax.axis_index("groups")
    me = lax.axis_index("seq")
    line, pair, core = me // 4, (me // 2) % 2, me % 2

    both = jnp.stack([audio_proj.T, vision_proj.T])
    keep = lax.dynamic_slice_in_dim(both, core * half, half, axis=2)
    give = lax.dynamic_slice_in_dim(both, (1 - core) * half, half, axis=2)
    got = flip(give, 1, devices)
    own = jnp.concatenate(
        [jnp.where(core == 0, keep, got), jnp.where(core == 0, got, keep)], axis=1
    )
    mine = jnp.where(group == 0, own[0], own[1])
    other = jnp.where(group == 0, own[1], own[0])

    ids = route_ids[:, 0]
    split = grad_rows.reshape(rows, lines, 2, 2 * k)
    near = jnp.where(pair == 0, split[:, :, 0], split[:, :, 1]).reshape(rows, lines * 2 * k)
    away = jnp.where(pair == 0, split[:, :, 1], split[:, :, 0]).reshape(rows, lines * 2 * k)
    partner = flip(away, 2, devices)
    far = flip(jnp.concatenate([near, partner]), 1, devices)
    pair_ids = flip(ids, 2, devices)
    far_ids = flip(jnp.concatenate([ids, pair_ids]), 1, devices)
    all_ids = jnp.concatenate([ids, pair_ids, far_ids])
    masks = (all_ids // devices == group).astype(jnp.int32)[:, None]

    outs = (
        jax.ShapeDtypeStruct((2 * rows, half), F32),
        jax.ShapeDtypeStruct((2 * rows, half), BF16),
    )
    if lines == 4:
        right1 = along(mine, [(0, 1), (1, 2), (2, 3)])
        left1 = along(mine, [(1, 0), (2, 1), (3, 2)])
        two_mid = along(jnp.where(line == 1, right1, left1), [(1, 2), (2, 1)])
        two_end = along(jnp.where(line == 1, left1, right1), [(2, 3), (1, 0)])
        three = along(two_mid, [(2, 3), (1, 0)])
        parts = [
            (mine, other),
            (right1, across(right1, [1, 2, 3], devices)),
            (left1, across(left1, [0, 1, 2], devices)),
            (two_mid, across(two_mid, [1, 2], devices)),
            (two_end, across(two_end, [0, 3], devices)),
            (three, across(three, [0, 3], devices)),
        ]
        scratch = [pltpu.VMEM((8 * k, half), BF16)] * 2 + [pltpu.SemaphoreType.DMA((8,))]
        kept, sent = call(product_line, outs, [SM] + [VM] * 4 + [ANY] * 12, scratch)(
            line.reshape(1), masks, near, partner, far, *[p[0] for p in parts], *[p[1] for p in parts]
        )
    else:
        groups = [[place(a, p, c) for a in range(lines)] for p in range(2) for c in range(2)]
        mine_w = lax.all_gather(mine, "seq", axis=0, tiled=True, axis_index_groups=groups)
        other_w = lax.all_gather(other, "seq", axis=0, tiled=True, axis_index_groups=groups)
        kept, sent = call(product_plain, outs, [VM] * 6)(masks, near, partner, far, mine_w, other_w)
    taken = flip(sent, 2, devices)

    src_ids = jnp.concatenate([ids, far_ids[:rows]])
    src_core = jnp.concatenate([jnp.full((rows,), core), jnp.full((rows,), 1 - core)])
    base = (src_ids % devices) * (4 * cap) + src_core * (2 * cap) + (src_ids // devices) * cap
    packed = call(pack, jax.ShapeDtypeStruct((4 * rows, half), BF16), [VM] * 4)(
        base[:, None], base[None, :], kept, taken
    )
    arrived = lax.all_to_all(packed.reshape(devices, 4 * cap, half), "seq", 0, 0, tiled=True)
    arrived = arrived.reshape(devices // 2, 2, 2, 2, cap, half)
    if cap % 16 != 0:
        arrived = arrived.transpose(1, 3, 0, 2, 4, 5).reshape(1, 2, 1, 2, rows, half)

    audio_grad, vision_grad, gains = call(
        norms,
        (
            jax.ShapeDtypeStruct((rows, enc), BF16),
            jax.ShapeDtypeStruct((rows, enc), BF16),
            jax.ShapeDtypeStruct((2, enc), F32),
        ),
        [VM] * 5,
    )(arrived, audio_states, vision_states, audio_gain[None, :], vision_gain[None, :])
    bit = 1
    while bit < devices:
        gains = gains + flip(gains, bit, devices)
        bit *= 2
    return (audio_grad, vision_grad, gains)


def solution(mesh):
    placed = (
        P(("groups", "seq"), None),
        P(("groups", "seq"), None),
        P(None, "seq"),
        P(None, "seq"),
        P(("groups", "seq"), None),
        P(("groups", "seq"), None),
        P(),
        P(),
    )
    return jax.shard_map(
        on_device,
        mesh=mesh,
        in_specs=placed,
        out_specs=(P(("groups", "seq"), None), P(("groups", "seq"), None), P("groups", None)),
        check_vma=False,
    )
```

```python
import functools

import jax
import jax.numpy as jnp
from jax import lax
from jax.experimental import pallas as pl
from jax.experimental.pallas import tpu as pltpu
from jax.sharding import PartitionSpec as P

F32 = jnp.float32
BF16 = jnp.bfloat16
BOTH = ("groups", "seq")
BIG = 48 * 1024 * 1024
VM = pl.BlockSpec(memory_space=pltpu.VMEM)
SM = pl.BlockSpec(memory_space=pltpu.SMEM)
ANY = pl.BlockSpec(memory_space=pl.ANY)


def flip(value, bits, devices):
    return lax.ppermute(value, "seq", [(i, i ^ bits) for i in range(devices)])


def spot(p, low, devices):
    group, line = (0, p) if p < 4 else (1, 7 - p)
    return group * devices + line * 4 + low


def cycle(value, moves, devices):
    pairs = [(spot(a, w, devices), spot(b, w, devices)) for a, b in moves for w in range(4)]
    return lax.ppermute(value, BOTH, pairs)


def gather_cycle(block, p, devices):
    fwd, bwd = [block], [block]
    for k in (1, 2, 3):
        up = [(a, (a + 1) % 8) for a in range(8)]
        down = [(a, (a - 1) % 8) for a in range(8)]
        if k == 3:
            up = [(a, b) for a, b in up if (b - k) % 8 != 7 - b]
            down = [(a, b) for a, b in down if (b + k) % 8 != 7 - b]
        fwd.append(cycle(fwd[-1], up, devices))
        bwd.append(cycle(bwd[-1], down, devices))
    first = (p % 4 == 0) | (p % 4 == 1)
    inner = cycle(jnp.where(first, bwd[1], fwd[1]), [(a, 7 - a) for a in (1, 2, 5, 6)], devices)
    outer = cycle(jnp.where(first, bwd[3], fwd[3]), [(a, 7 - a) for a in (0, 3, 4, 7)], devices)
    return fwd[1:] + bwd[1:] + [inner, outer]


def cut(place, a_ref, v_ref, keep, to_core, to_pair, to_both, sems):
    pair, core = place[0], place[1]
    half = keep.shape[1]
    near = pl.ds(pl.multiple_of(pair * half, 128), half)
    away = pl.ds(pl.multiple_of((1 - pair) * half, 128), half)
    for here in range(2):
        mine, other = (a_ref, v_ref) if here == 0 else (v_ref, a_ref)

        @pl.when(core == here)
        def _():
            pltpu.make_async_copy(other.at[:, near], to_core, sems.at[0]).start()
            pltpu.make_async_copy(mine.at[:, near], keep, sems.at[1]).start()
            pltpu.make_async_copy(mine.at[:, away], to_pair, sems.at[2]).start()
            pltpu.make_async_copy(other.at[:, away], to_both, sems.at[3]).start()

    for i, out in enumerate((to_core, keep, to_pair, to_both)):
        pltpu.make_async_copy(a_ref.at[:, near], out, sems.at[i]).wait()


def one_hot_pack(lhs, w, base_col, base_row, source, out):
    rows = lhs[0].shape[0]
    devices, sources, cap, half = out.shape
    first = lax.broadcasted_iota(jnp.int32, (rows, rows), 0)
    second = lax.broadcasted_iota(jnp.int32, (rows, rows), 1)
    slots = lax.broadcasted_iota(jnp.int32, (devices * cap, rows), 0)
    for s in range(4):
        col = base_col[s * rows : (s + 1) * rows, :]
        row = base_row[:, s * rows : (s + 1) * rows]
        same = jnp.logical_and(col == row, first < second)
        count = jnp.sum(same.astype(F32), axis=0, keepdims=True).astype(jnp.int32)
        pick = (slots == row + count).astype(F32).astype(BF16)
        up = jnp.dot(lhs[s][...], w[...], preferred_element_type=F32).astype(BF16)
        packed = jnp.dot(pick, up, preferred_element_type=F32).astype(BF16)
        out[:, source[s]] = packed.reshape(devices, cap, half)


def product_cycle(*refs):
    place, source, base_col, base_row = refs[:4]
    lhs, parts = refs[4:8], refs[8:28]
    out, w, sems = refs[28:]
    deep = parts[0].shape[0]
    p, x = place[0], place[1]

    def spread(op):
        for chain in range(2):
            own, pair, f1, f2, f3, b1, b2, b3, inner, outer = parts[chain * 10 : chain * 10 + 10]
            which = jnp.where(chain == 0, x, 1 - x)

            def move(ref, q, i):
                group = q // 4
                line = jnp.where(group == 0, q, 7 - q)
                start = pl.multiple_of(((line * 2 + which) * 2 + group) * deep, 16)
                op(pltpu.make_async_copy(ref, w.at[pl.ds(start, deep)], sems.at[chain * 8 + i]))

            move(own, p, 0)
            move(pair, 7 - p, 1)
            far = (p + 4) % 8
            ends = p % 4
            for i, (ref, step) in enumerate(((f1, 7), (f2, 6), (f3, 5), (b1, 1), (b2, 2), (b3, 3))):
                q = (p + step) % 8

                @pl.when(q != 7 - p)
                def _():
                    move(ref, q, 2 + i if i < 5 else 7)

            spare = jnp.where(ends == 0, 2, jnp.where(ends == 1, 4, jnp.where(ends == 2, 7, 5)))

            @pl.when((ends == 0) | (ends == 3))
            def _():
                move(outer, far, spare)

            @pl.when((ends == 1) | (ends == 2))
            def _():
                move(inner, far, spare)

    spread(lambda c: c.start())
    spread(lambda c: c.wait())
    one_hot_pack(lhs, w, base_col, base_row, source, out)


def product_plain(base_col, base_row, l0, l1, l2, l3, w, out):
    rows = l0.shape[0]
    total = 4 * rows
    first = lax.broadcasted_iota(jnp.int32, (total, total), 0)
    second = lax.broadcasted_iota(jnp.int32, (total, total), 1)
    same = jnp.logical_and(base_col[...] == base_row[...], first < second)
    slot = base_row[...] + jnp.sum(same.astype(F32), axis=0, keepdims=True).astype(jnp.int32)
    slots = lax.broadcasted_iota(jnp.int32, (total, rows), 0)
    acc = jnp.zeros(out.shape, F32)
    for s, ref in enumerate((l0, l1, l2, l3)):
        pick = (slots == slot[:, s * rows : (s + 1) * rows]).astype(F32).astype(BF16)
        up = jnp.dot(ref[...], w[...], preferred_element_type=F32).astype(BF16)
        acc = acc + jnp.dot(pick, up, preferred_element_type=F32)
    out[...] = acc.astype(BF16)


def norms(recv, a_states, v_states, a_gain, v_gain, a_out, v_out, gains):
    rows, width = a_states.shape
    half = width // 2
    inv = 1.0 / width

    def upstream(h, m):
        return recv[:, h, m].reshape(rows, half).astype(F32)

    def cols(h):
        return slice(h * half, (h + 1) * half)

    h = a_states[...].astype(F32)
    mu = jnp.sum(h, axis=1, keepdims=True) * inv
    centred = h - mu
    scale = lax.rsqrt(jnp.sum(centred * centred, axis=1, keepdims=True) * inv + 1e-5)
    normed = centred * scale
    ps, pn, parts = 0.0, 0.0, []
    for k in range(2):
        u = upstream(k, 0)
        n = normed[:, cols(k)]
        p = u * a_gain[:, cols(k)]
        ps = ps + jnp.sum(p, axis=1, keepdims=True)
        pn = pn + jnp.sum(p * n, axis=1, keepdims=True)
        gains[0:1, cols(k)] = jnp.sum(u * n, axis=0, keepdims=True)
        parts.append((p, n))
    for k in range(2):
        p, n = parts[k]
        a_out[:, cols(k)] = (scale * (p - ps * inv - n * (pn * inv))).astype(BF16)

    h = v_states[...].astype(F32)
    scale = lax.rsqrt(jnp.sum(h * h, axis=1, keepdims=True) * inv + 1e-6)
    normed = h * scale
    pn, parts = 0.0, []
    for k in range(2):
        u = upstream(k, 1)
        n = normed[:, cols(k)]
        p = u * v_gain[:, cols(k)]
        pn = pn + jnp.sum(p * n, axis=1, keepdims=True)
        gains[1:2, cols(k)] = jnp.sum(u * n, axis=0, keepdims=True)
        parts.append((p, n))
    for k in range(2):
        p, n = parts[k]
        v_out[:, cols(k)] = (scale * (p - n * (pn * inv))).astype(BF16)


def call(body, outs, specs, scratch=(), out_spec=VM):
    return pl.pallas_call(
        body,
        out_shape=outs,
        in_specs=specs,
        out_specs=jax.tree.map(lambda _: out_spec, outs),
        scratch_shapes=list(scratch),
        compiler_params=pltpu.CompilerParams(vmem_limit_bytes=BIG),
    )


def on_device(
    grad_rows,
    route_ids,
    audio_proj,
    vision_proj,
    audio_states,
    vision_states,
    audio_gain,
    vision_gain,
):
    devices = lax.axis_size("seq")
    lines = devices // 4
    rows, width = grad_rows.shape
    enc, k = audio_proj.shape
    half = enc // 2
    cap = rows // devices
    group = lax.axis_index("groups")
    me = lax.axis_index("seq")
    line, pair, core = me // 4, (me // 2) % 2, me % 2

    block = jax.ShapeDtypeStruct((k, half), BF16)
    if lines == 4:
        keep, to_core, to_pair, to_both = call(
            cut, (block,) * 4, [SM, ANY, ANY], [pltpu.SemaphoreType.DMA((4,))], ANY
        )(jnp.stack([pair, core]), audio_proj.T, vision_proj.T)
    else:
        both = jnp.stack([audio_proj.T, vision_proj.T]).reshape(2, k, 2, half)
        pick = lambda m, h: both[m, :, h]
        keep, to_core = pick(core, pair), pick(1 - core, pair)
        to_pair, to_both = pick(core, 1 - pair), pick(1 - core, 1 - pair)
    from_core = flip(to_core, 1, devices)
    from_pair = flip(to_pair, 2, devices)
    from_both = flip(to_both, 3, devices)

    r_pair = flip(grad_rows, 2, devices)
    r_core = flip(grad_rows, 1, devices)
    r_both = flip(r_pair, 1, devices)
    ids = route_ids[:, 0]
    i_pair = flip(ids, 2, devices)
    i_far = flip(jnp.concatenate([ids, i_pair]), 1, devices)
    all_ids = jnp.concatenate([ids, i_pair, i_far])
    lhs = (grad_rows, r_pair, r_core, r_both)
    low = me % 4
    source = jnp.stack([low, low ^ 2, low ^ 1, low ^ 3])
    named = all_ids // devices == core

    if lines == 4:
        p = jnp.where(group == 0, line, 7 - line)
        straight = core == group
        block1 = jnp.where(straight, keep, from_core)
        mirror1 = jnp.where(straight, from_core, keep)
        block2 = jnp.where(straight, from_pair, from_both)
        mirror2 = jnp.where(straight, from_both, from_pair)
        parts1 = [block1, mirror1] + gather_cycle(block1, p, devices)
        parts2 = [block2, mirror2] + gather_cycle(block2, p, devices)
        base = jnp.where(named, all_ids % devices * cap, -(2 * rows))
        packed = call(
            product_cycle,
            jax.ShapeDtypeStruct((devices, 4, cap, half), BF16),
            [SM, SM] + [VM] * 6 + [ANY] * 20,
            [pltpu.VMEM((width, half), BF16), pltpu.SemaphoreType.DMA((16,))],
        )(jnp.stack([p, pair]), source, base[:, None], base[None, :], *lhs, *parts1, *parts2)
        packed = packed.reshape(devices, 4 * cap, half)
    else:
        straight = jnp.stack([keep, from_pair, from_core, from_both])
        plane = jnp.zeros_like(straight).at[source].set(straight)
        ranks = [[a * 4 + w for a in range(lines)] for w in range(4)]
        w = lax.all_gather(plane.reshape(4 * k, half), "seq", axis=0, tiled=True, axis_index_groups=ranks)
        where_from = jnp.repeat(source, rows)
        base = jnp.where(named, (all_ids % devices * 4 + where_from) * cap, -(8 * rows))
        packed = call(product_plain, jax.ShapeDtypeStruct((4 * rows, half), BF16), [VM] * 7)(
            base[:, None], base[None, :], *lhs, w
        )
        packed = packed.reshape(devices, 4 * cap, half)

    arrived = lax.all_to_all(packed, "seq", 0, 0, tiled=True)
    arrived = arrived.reshape(lines, 2, 2, 4, cap, half)
    if cap % 16 != 0:
        arrived = arrived.transpose(1, 2, 0, 3, 4, 5).reshape(1, 2, 2, 1, rows, half)

    audio_grad, vision_grad, gains = call(
        norms,
        (
            jax.ShapeDtypeStruct((rows, enc), BF16),
            jax.ShapeDtypeStruct((rows, enc), BF16),
            jax.ShapeDtypeStruct((2, enc), F32),
        ),
        [VM] * 5,
    )(arrived, audio_states, vision_states, audio_gain[None, :], vision_gain[None, :])
    bit = 1
    while bit < devices:
        near = flip(gains, bit, devices)
        if 2 * bit < devices:
            far = flip(gains, 2 * bit, devices) + flip(gains, 3 * bit, devices)
            gains = (gains + near) + far
        else:
            gains = gains + near
        bit *= 4
    return (audio_grad, vision_grad, gains)


def solution(mesh):
    placed = (
        P(("groups", "seq"), None),
        P(("groups", "seq"), None),
        P(None, "seq"),
        P(None, "seq"),
        P(("groups", "seq"), None),
        P(("groups", "seq"), None),
        P(),
        P(),
    )
    return jax.shard_map(
        on_device,
        mesh=mesh,
        in_specs=placed,
        out_specs=(P(("groups", "seq"), None), P(("groups", "seq"), None), P("groups", None)),
        check_vma=False,
    )
```

```python
import functools

import jax
import jax.numpy as jnp
from jax import lax
from jax.experimental import pallas as pl
from jax.experimental.pallas import tpu as pltpu
from jax.sharding import PartitionSpec as P

F32 = jnp.float32
BF16 = jnp.bfloat16
BOTH = ("groups", "seq")
BIG = 24 * 1024 * 1024
VM = pl.BlockSpec(memory_space=pltpu.VMEM)
SM = pl.BlockSpec(memory_space=pltpu.SMEM)
ANY = pl.BlockSpec(memory_space=pl.ANY)


def flip(value, bits, devices):
    return lax.ppermute(value, "seq", [(i, i ^ bits) for i in range(devices)])


def spot(p, low, devices):
    group, line = (0, p) if p < 4 else (1, 7 - p)
    return group * devices + line * 4 + low


def cycle(value, moves, devices):
    pairs = [(spot(a, w, devices), spot(b, w, devices)) for a, b in moves for w in range(4)]
    return lax.ppermute(value, BOTH, pairs)


def after(value, *others):
    return lax.optimization_barrier((value,) + others)[0]


def step(fwd, bwd, k, devices):
    up = [(a, (a + 1) % 8) for a in range(8)]
    down = [(a, (a - 1) % 8) for a in range(8)]
    if k == 3:
        up = [(a, b) for a, b in up if (b - k) % 8 != 7 - b]
        down = [(a, b) for a, b in down if (b + k) % 8 != 7 - b]
    return cycle(fwd, up, devices), cycle(bwd, down, devices)


def swap(fwd, bwd, p, spots, devices):
    first = (p % 4 == 0) | (p % 4 == 1)
    return cycle(jnp.where(first, bwd, fwd), [(a, 7 - a) for a in spots], devices)


def cut(place, a_ref, v_ref, keep, to_core, to_pair, to_both, sems):
    pair, core = place[0], place[1]
    half = keep.shape[1]
    near = pl.ds(pl.multiple_of(pair * half, 128), half)
    away = pl.ds(pl.multiple_of((1 - pair) * half, 128), half)
    for here in range(2):
        mine, other = (a_ref, v_ref) if here == 0 else (v_ref, a_ref)

        @pl.when(core == here)
        def _():
            pltpu.make_async_copy(other.at[:, near], to_core, sems.at[0]).start()
            pltpu.make_async_copy(mine.at[:, near], keep, sems.at[1]).start()
            pltpu.make_async_copy(mine.at[:, away], to_pair, sems.at[2]).start()
            pltpu.make_async_copy(other.at[:, away], to_both, sems.at[3]).start()

    for i, out in enumerate((to_core, keep, to_pair, to_both)):
        pltpu.make_async_copy(a_ref.at[:, near], out, sems.at[i]).wait()


def columns(line, width):
    return pl.ds(pl.multiple_of(line * (width // 4), 128), width // 4)


def line_of(q):
    return jnp.where(q < 4, q, 7 - q)


def load_rows(lhs, lines, buf, sem):
    rows, width = lhs[0].shape
    copies = []
    for j, line in enumerate(lines):
        for s, ref in enumerate(lhs):
            to = buf.at[pl.ds(s * rows, rows), pl.ds(j * (width // 4), width // 4)]
            copies.append(pltpu.make_async_copy(ref.at[:, columns(line, width)], to, sem.at[8 + j * len(lhs) + s]))
    return copies


def second_line(line):
    return jnp.where((line == 0) | (line == 2), 1, 2)


def last_lines(line):
    return jnp.where(line == 0, 2, 0), jnp.where(line == 3, 1, 3)


def near_half(*refs):
    place = refs[0]
    parts, lhs = refs[1:15], refs[15:-4]
    out, buf, w, sems = refs[-4:]
    deep = parts[0].shape[0]
    p, x = place[0], place[1]
    ends = p % 4
    line = line_of(p)
    second = second_line(line)
    copies = load_rows(lhs, (line, second), buf, sems)
    for c in copies:
        c.start()

    def move(ref, q, slot, which, i):
        start = pl.multiple_of(((slot * 2 + which) * 2 + q // 4) * deep, 16)
        return pltpu.make_async_copy(ref, w.at[pl.ds(start, deep)], sems.at[slot * 4 + i])

    for chain in range(2):
        own, pair, f1, b1, f2, b2, inner = parts[chain * 7 : chain * 7 + 7]
        which = jnp.where(chain == 0, x, 1 - x)
        move(own, p, 0, which, 2 * chain).start()
        move(pair, 7 - p, 0, which, 2 * chain + 1).start()
        for case, one, two in ((0, (b1, 1), (f2, 6)), (1, (b1, 1), (inner, 4)), (2, (f1, 7), (inner, 4)), (3, (f1, 7), (b2, 2))):

            @pl.when(ends == case)
            def _():
                for i, (ref, step) in enumerate((one, two)):
                    move(ref, (p + step) % 8, 1, which, 2 * chain + i).start()

    acc = None
    for slot in range(2):
        for c in copies[slot * len(lhs) : (slot + 1) * len(lhs)]:
            c.wait()
        for i in range(4):
            move(parts[0], p, slot, x, i).wait()
        span = slice(slot * 4 * deep, (slot + 1) * 4 * deep)
        part = jnp.dot(buf[:, span], w[span, :], preferred_element_type=F32)
        acc = part if acc is None else acc + part
    out[...] = acc


def far_half(*refs):
    place, source, base_col, base_row, acc_near, acc_far = refs[:6]
    parts, lhs = refs[6:20], refs[20:24]
    out, buf, w, sems = refs[24:]
    deep = parts[0].shape[0]
    rows = lhs[0].shape[0]
    devices, sources, cap, half = out.shape
    p, x = place[0], place[1]
    ends = p % 4
    line = line_of(p)
    third, fourth = last_lines(line)
    copies = load_rows(lhs, (third, fourth), buf, sems)
    for c in copies:
        c.start()

    def move(ref, q, which, i):
        slot = jnp.where(line_of(q) == third, 0, 1)
        start = pl.multiple_of(((slot * 2 + which) * 2 + q // 4) * deep, 16)
        return pltpu.make_async_copy(ref, w.at[pl.ds(start, deep)], sems.at[i])

    for chain in range(2):
        f1, f2, f3, b1, b2, b3, outer = parts[chain * 7 : chain * 7 + 7]
        which = jnp.where(chain == 0, x, 1 - x)
        f1, f2, f3, b1, b2, b3 = (f1, 7), (f2, 6), (f3, 5), (b1, 1), (b2, 2), (b3, 3)
        outer = (outer, 4)
        for case, takes in enumerate(((b2, f3, b3, outer), (f1, f2, b2, b3), (f2, f3, b1, b2), (f2, f3, b3, outer))):

            @pl.when(ends == case)
            def _():
                for i, (ref, step) in enumerate(takes):
                    move(ref, (p + step) % 8, which, 4 * chain + i).start()

    first = lax.broadcasted_iota(jnp.int32, (rows, rows), 0)
    later = lax.broadcasted_iota(jnp.int32, (rows, rows), 1)
    slots = lax.broadcasted_iota(jnp.int32, (devices * cap, rows), 0)
    picks = []
    for s in range(4):
        col = base_col[s * rows : (s + 1) * rows, :]
        row = base_row[:, s * rows : (s + 1) * rows]
        same = jnp.logical_and(col == row, first < later)
        count = jnp.sum(same.astype(F32), axis=0, keepdims=True).astype(jnp.int32)
        picks.append((slots == row + count).astype(F32).astype(BF16))
    for c in copies:
        c.wait()
    for i in range(8):
        move(parts[0], p, x, i).wait()
    for s in range(4):
        acc = acc_near if s % 2 == 0 else acc_far
        at = slice((s // 2) * rows, (s // 2 + 1) * rows)
        up = acc[at, :] + jnp.dot(buf[s * rows : (s + 1) * rows, :], w[...], preferred_element_type=F32)
        packed = jnp.dot(picks[s], up.astype(BF16), preferred_element_type=F32).astype(BF16)
        out[:, source[s]] = packed.reshape(devices, cap, half)


def product_plain(base_col, base_row, l0, l1, l2, l3, w, out):
    rows = l0.shape[0]
    total = 4 * rows
    first = lax.broadcasted_iota(jnp.int32, (total, total), 0)
    second = lax.broadcasted_iota(jnp.int32, (total, total), 1)
    same = jnp.logical_and(base_col[...] == base_row[...], first < second)
    slot = base_row[...] + jnp.sum(same.astype(F32), axis=0, keepdims=True).astype(jnp.int32)
    slots = lax.broadcasted_iota(jnp.int32, (total, rows), 0)
    acc = jnp.zeros(out.shape, F32)
    for s, ref in enumerate((l0, l1, l2, l3)):
        pick = (slots == slot[:, s * rows : (s + 1) * rows]).astype(F32).astype(BF16)
        up = jnp.dot(ref[...], w[...], preferred_element_type=F32).astype(BF16)
        acc = acc + jnp.dot(pick, up, preferred_element_type=F32)
    out[...] = acc.astype(BF16)


def norms(recv, a_states, v_states, a_gain, v_gain, a_out, v_out, gains):
    rows, width = a_states.shape
    half = width // 2
    inv = 1.0 / width

    def upstream(h, m):
        return recv[:, h, m].reshape(rows, half).astype(F32)

    def cols(h):
        return slice(h * half, (h + 1) * half)

    h = a_states[...].astype(F32)
    mu = jnp.sum(h, axis=1, keepdims=True) * inv
    centred = h - mu
    scale = lax.rsqrt(jnp.sum(centred * centred, axis=1, keepdims=True) * inv + 1e-5)
    normed = centred * scale
    ps, pn, parts = 0.0, 0.0, []
    for k in range(2):
        u = upstream(k, 0)
        n = normed[:, cols(k)]
        p = u * a_gain[:, cols(k)]
        ps = ps + jnp.sum(p, axis=1, keepdims=True)
        pn = pn + jnp.sum(p * n, axis=1, keepdims=True)
        gains[0:1, cols(k)] = jnp.sum(u * n, axis=0, keepdims=True)
        parts.append((p, n))
    for k in range(2):
        p, n = parts[k]
        a_out[:, cols(k)] = (scale * (p - ps * inv - n * (pn * inv))).astype(BF16)

    h = v_states[...].astype(F32)
    scale = lax.rsqrt(jnp.sum(h * h, axis=1, keepdims=True) * inv + 1e-6)
    normed = h * scale
    pn, parts = 0.0, []
    for k in range(2):
        u = upstream(k, 1)
        n = normed[:, cols(k)]
        p = u * v_gain[:, cols(k)]
        pn = pn + jnp.sum(p * n, axis=1, keepdims=True)
        gains[1:2, cols(k)] = jnp.sum(u * n, axis=0, keepdims=True)
        parts.append((p, n))
    for k in range(2):
        p, n = parts[k]
        v_out[:, cols(k)] = (scale * (p - n * (pn * inv))).astype(BF16)


def call(body, outs, specs, scratch=(), out_spec=VM):
    return pl.pallas_call(
        body,
        out_shape=outs,
        in_specs=specs,
        out_specs=jax.tree.map(lambda _: out_spec, outs),
        scratch_shapes=list(scratch),
        compiler_params=pltpu.CompilerParams(vmem_limit_bytes=BIG),
    )


def on_device(
    grad_rows,
    route_ids,
    audio_proj,
    vision_proj,
    audio_states,
    vision_states,
    audio_gain,
    vision_gain,
):
    devices = lax.axis_size("seq")
    lines = devices // 4
    rows, width = grad_rows.shape
    enc, k = audio_proj.shape
    half = enc // 2
    cap = rows // devices
    group = lax.axis_index("groups")
    me = lax.axis_index("seq")
    line, pair, core = me // 4, (me // 2) % 2, me % 2

    block = jax.ShapeDtypeStruct((k, half), BF16)
    if lines == 4:
        keep, to_core, to_pair, to_both = call(
            cut, (block,) * 4, [SM, ANY, ANY], [pltpu.SemaphoreType.DMA((4,))], ANY
        )(jnp.stack([pair, core]), audio_proj.T, vision_proj.T)
    else:
        both = jnp.stack([audio_proj.T, vision_proj.T]).reshape(2, k, 2, half)
        pick = lambda m, h: both[m, :, h]
        keep, to_core = pick(core, pair), pick(1 - core, pair)
        to_pair, to_both = pick(core, 1 - pair), pick(1 - core, 1 - pair)
    from_core = flip(to_core, 1, devices)
    from_pair = flip(to_pair, 2, devices)
    from_both = flip(to_both, 3, devices)

    r_pair = flip(after(grad_rows, from_pair, from_both), 2, devices)
    r_core = flip(grad_rows, 1, devices)
    r_both = flip(r_pair, 1, devices)
    ids = route_ids[:, 0]
    i_pair = flip(ids, 2, devices)
    i_far = flip(jnp.concatenate([ids, i_pair]), 1, devices)
    all_ids = jnp.concatenate([ids, i_pair, i_far])
    lhs = (grad_rows, r_pair, r_core, r_both)
    low = me % 4
    source = jnp.stack([low, low ^ 2, low ^ 1, low ^ 3])
    named = all_ids // devices == core

    if lines == 4:
        p = jnp.where(group == 0, line, 7 - line)
        straight = core == group
        block1 = jnp.where(straight, keep, from_core)
        mirror1 = jnp.where(straight, from_core, keep)
        f1, b1 = step(block1, block1, 1, devices)
        from_pair, from_both = after((from_pair, from_both), f1)
        block2 = jnp.where(straight, from_pair, from_both)
        mirror2 = jnp.where(straight, from_both, from_pair)
        chains = []
        for block, mirror, got in ((block1, mirror1, (f1, b1)), (block2, mirror2, None)):
            f1, b1 = got or step(block, block, 1, devices)
            f2, b2 = step(f1, b1, 2, devices)
            inner = swap(f1, b1, p, (1, 2, 5, 6), devices)
            f3, b3 = step(f2, b2, 3, devices)
            outer = swap(f3, b3, p, (0, 3, 4, 7), devices)
            chains.append((block, mirror, f1, b1, f2, b2, f3, b3, inner, outer))
        early = [v for c in chains for v in (c[0], c[1], c[2], c[3], c[4], c[5], c[8])]
        late = [v for c in chains for v in (c[2], c[4], c[6], c[3], c[5], c[7], c[9])]
        spots = jnp.stack([p, pair])
        acc = jax.ShapeDtypeStruct((2 * rows, half), F32)

        def scratch(n):
            return [
                pltpu.VMEM((n * rows, width // 2), BF16),
                pltpu.VMEM((width // 2, half), BF16),
                pltpu.SemaphoreType.DMA((16,)),
            ]

        near = [
            call(near_half, acc, [SM] + [ANY] * 16, scratch(2))(spots, *early, *pair_of)
            for pair_of in ((lhs[0], lhs[2]), (lhs[1], lhs[3]))
        ]
        base = jnp.where(named, all_ids % devices * cap, -(2 * rows))
        packed = call(
            far_half,
            jax.ShapeDtypeStruct((devices, 4, cap, half), BF16),
            [SM, SM] + [VM] * 4 + [ANY] * 18,
            scratch(4),
        )(spots, source, base[:, None], base[None, :], *near, *late, *lhs)
        packed = packed.reshape(devices, 4 * cap, half)
    else:
        straight = jnp.stack([keep, from_pair, from_core, from_both])
        plane = jnp.zeros_like(straight).at[source].set(straight)
        ranks = [[a * 4 + w for a in range(lines)] for w in range(4)]
        w = lax.all_gather(plane.reshape(4 * k, half), "seq", axis=0, tiled=True, axis_index_groups=ranks)
        where_from = jnp.repeat(source, rows)
        base = jnp.where(named, (all_ids % devices * 4 + where_from) * cap, -(8 * rows))
        packed = call(product_plain, jax.ShapeDtypeStruct((4 * rows, half), BF16), [VM] * 7)(
            base[:, None], base[None, :], *lhs, w
        )
        packed = packed.reshape(devices, 4 * cap, half)

    arrived = lax.all_to_all(packed, "seq", 0, 0, tiled=True)
    arrived = arrived.reshape(lines, 2, 2, 4, cap, half)
    if cap % 16 != 0:
        arrived = arrived.transpose(1, 2, 0, 3, 4, 5).reshape(1, 2, 2, 1, rows, half)

    audio_grad, vision_grad, gains = call(
        norms,
        (
            jax.ShapeDtypeStruct((rows, enc), BF16),
            jax.ShapeDtypeStruct((rows, enc), BF16),
            jax.ShapeDtypeStruct((2, enc), F32),
        ),
        [VM] * 5,
    )(arrived, audio_states, vision_states, audio_gain[None, :], vision_gain[None, :])
    bit = 1
    while bit < devices:
        near = flip(gains, bit, devices)
        if 2 * bit < devices:
            far = flip(gains, 2 * bit, devices) + flip(gains, 3 * bit, devices)
            gains = (gains + near) + far
        else:
            gains = gains + near
        bit *= 4
    return (audio_grad, vision_grad, gains)


def solution(mesh):
    placed = (
        P(("groups", "seq"), None),
        P(("groups", "seq"), None),
        P(None, "seq"),
        P(None, "seq"),
        P(("groups", "seq"), None),
        P(("groups", "seq"), None),
        P(),
        P(),
    )
    return jax.shard_map(
        on_device,
        mesh=mesh,
        in_specs=placed,
        out_specs=(P(("groups", "seq"), None), P(("groups", "seq"), None), P("groups", None)),
        check_vma=False,
    )
```

```python
import functools

import jax
import jax.numpy as jnp
from jax import lax
from jax.experimental import pallas as pl
from jax.experimental.pallas import tpu as pltpu
from jax.sharding import PartitionSpec as P

F32 = jnp.float32
BF16 = jnp.bfloat16
BOTH = ("groups", "seq")
BIG = 24 * 1024 * 1024
WHOLE = 60 * 1024 * 1024
VM = pl.BlockSpec(memory_space=pltpu.VMEM)
SM = pl.BlockSpec(memory_space=pltpu.SMEM)
ANY = pl.BlockSpec(memory_space=pl.ANY)


def flip(value, bits, devices):
    return lax.ppermute(value, "seq", [(i, i ^ bits) for i in range(devices)])


def cross(value, bits, devices):
    pairs = [(g * devices + i, g * devices + (i ^ bits)) for g in range(2) for i in range(g, devices, 2)]
    return lax.ppermute(value, BOTH, pairs)


def spot(p, low, devices):
    group, line = (0, p) if p < 4 else (1, 7 - p)
    return group * devices + line * 4 + low


def cycle(value, moves, devices):
    pairs = [(spot(a, w, devices), spot(b, w, devices)) for a, b in moves for w in range(4)]
    return lax.ppermute(value, BOTH, pairs)


def after(value, *others):
    return lax.optimization_barrier((value,) + others)[0]


def step(fwd, bwd, k, devices):
    up = [(a, (a + 1) % 8) for a in range(8)]
    down = [(a, (a - 1) % 8) for a in range(8)]
    if k == 3:
        up = [(a, b) for a, b in up if (b - k) % 8 != 7 - b]
        down = [(a, b) for a, b in down if (b + k) % 8 != 7 - b]
    return cycle(fwd, up, devices), cycle(bwd, down, devices)


def swap(fwd, bwd, p, spots, devices):
    first = (p % 4 == 0) | (p % 4 == 1)
    return cycle(jnp.where(first, bwd, fwd), [(a, 7 - a) for a in spots], devices)


def cut(place, a_ref, v_ref, keep, to_core, to_pair, to_both, sems):
    pair, core = place[0], place[1]
    half = keep.shape[1]
    near = pl.ds(pl.multiple_of(pair * half, 128), half)
    away = pl.ds(pl.multiple_of((1 - pair) * half, 128), half)
    for here in range(2):
        mine, other = (a_ref, v_ref) if here == 0 else (v_ref, a_ref)

        @pl.when(core == here)
        def _():
            pltpu.make_async_copy(other.at[:, near], to_core, sems.at[0]).start()
            pltpu.make_async_copy(mine.at[:, near], keep, sems.at[1]).start()
            pltpu.make_async_copy(mine.at[:, away], to_pair, sems.at[2]).start()
            pltpu.make_async_copy(other.at[:, away], to_both, sems.at[3]).start()

    for i, out in enumerate((to_core, keep, to_pair, to_both)):
        pltpu.make_async_copy(a_ref.at[:, near], out, sems.at[i]).wait()


def columns(line, width):
    return pl.ds(pl.multiple_of(line * (width // 4), 128), width // 4)


def line_of(q):
    return jnp.where(q < 4, q, 7 - q)


def load_rows(lhs, lines, buf, sem):
    rows, width = lhs[0].shape
    copies = []
    for j, line in enumerate(lines):
        for s, ref in enumerate(lhs):
            to = buf.at[pl.ds(s * rows, rows), pl.ds(j * (width // 4), width // 4)]
            copies.append(pltpu.make_async_copy(ref.at[:, columns(line, width)], to, sem.at[16 + j * len(lhs) + s]))
    return copies


def second_line(line):
    return jnp.where((line == 0) | (line == 2), 1, 2)


def last_lines(line):
    return jnp.where(line == 0, 2, 0), jnp.where(line == 3, 1, 3)


def product_cycle(*refs):
    place, source, base_col, base_row = refs[:4]
    parts, lhs = refs[4:24], refs[24:28]
    out, buf, w, acc, sems = refs[28:]
    deep = parts[0].shape[0]
    rows = lhs[0].shape[0]
    devices, sources, cap, half = out.shape
    p, x = place[0], place[1]
    ends = p % 4
    line = line_of(p)
    second = second_line(line)
    third, fourth = last_lines(line)
    copies = load_rows(lhs, (line, second, third, fourth), buf, sems)

    def move(ref, q, slot, which, i):
        start = pl.multiple_of(((slot * 2 + which) * 2 + q // 4) * deep, 16)
        return pltpu.make_async_copy(ref, w.at[pl.ds(start, deep)], sems.at[i])

    for j in range(2):
        for c in copies[8 * j : 8 * j + 8]:
            c.start()
        for chain in range(2):
            own, mirror, f1, f2, f3, b1, b2, b3, inner, outer = parts[chain * 10 : chain * 10 + 10]
            which = jnp.where(chain == 0, x, 1 - x)
            f1, f2, f3, b1, b2, b3 = (f1, 7), (f2, 6), (f3, 5), (b1, 1), (b2, 2), (b3, 3)
            inner, outer = (inner, 4), (outer, 4)
            if j == 0:
                move(own, p, 0, which, 4 * chain).start()
            for case in range(4):

                @pl.when(ends == case)
                def _():
                    if j == 0:
                        ref = mirror if chain == 0 else (f1[0], mirror, mirror, b1[0])[case]
                        move(ref, 7 - p, 0, which, 4 * chain + 1).start()
                        takes = ((b1, f2), (b1, inner), (f1, inner), (f1, b2))[case]
                        for i, (ref, step) in enumerate(takes):
                            move(ref, (p + step) % 8, 1, which, 4 * chain + 2 + i).start()
                    else:
                        takes = ((b2, f3, b3, outer), (f1, f2, b2, b3), (f2, f3, b1, b2), (f2, f3, b3, outer))[case]
                        for i, (ref, step) in enumerate(takes):
                            q = (p + step) % 8
                            slot = jnp.where(line_of(q) == third, 2, 3)
                            move(ref, q, slot, which, 8 + 4 * chain + i).start()

    first = lax.broadcasted_iota(jnp.int32, (rows, rows), 0)
    later = lax.broadcasted_iota(jnp.int32, (rows, rows), 1)
    slots = lax.broadcasted_iota(jnp.int32, (devices * cap, rows), 0)
    picks = []
    for s in range(4):
        col = base_col[s * rows : (s + 1) * rows, :]
        row = base_row[:, s * rows : (s + 1) * rows]
        same = jnp.logical_and(col == row, first < later)
        count = jnp.sum(same.astype(F32), axis=0, keepdims=True).astype(jnp.int32)
        picks.append((slots == row + count).astype(F32).astype(BF16))
    for j in range(2):
        for c in copies[8 * j : 8 * j + 8]:
            c.wait()
        for i in range(8):
            move(parts[0], p, 0, x, 8 * j + i).wait()
        span = slice(j * 8 * deep, (j + 1) * 8 * deep)
        if j == 0:
            acc[...] = jnp.dot(buf[:, span], w[span, :], preferred_element_type=F32)
    for s in range(4):
        at = slice(s * rows, (s + 1) * rows)
        up = acc[at, :] + jnp.dot(buf[at, span], w[span, :], preferred_element_type=F32)
        packed = jnp.dot(picks[s], up.astype(BF16), preferred_element_type=F32).astype(BF16)
        out[:, source[s]] = packed.reshape(devices, cap, half)


def product_plain(base_col, base_row, l0, l1, l2, l3, w, out):
    rows = l0.shape[0]
    total = 4 * rows
    first = lax.broadcasted_iota(jnp.int32, (total, total), 0)
    second = lax.broadcasted_iota(jnp.int32, (total, total), 1)
    same = jnp.logical_and(base_col[...] == base_row[...], first < second)
    slot = base_row[...] + jnp.sum(same.astype(F32), axis=0, keepdims=True).astype(jnp.int32)
    slots = lax.broadcasted_iota(jnp.int32, (total, rows), 0)
    acc = jnp.zeros(out.shape, F32)
    for s, ref in enumerate((l0, l1, l2, l3)):
        pick = (slots == slot[:, s * rows : (s + 1) * rows]).astype(F32).astype(BF16)
        up = jnp.dot(ref[...], w[...], preferred_element_type=F32).astype(BF16)
        acc = acc + jnp.dot(pick, up, preferred_element_type=F32)
    out[...] = acc.astype(BF16)


def norms(recv, a_states, v_states, a_gain, v_gain, a_out, v_out, gains):
    rows, width = a_states.shape
    half = width // 2
    inv = 1.0 / width

    def upstream(h, m):
        return recv[:, h, m].reshape(rows, half).astype(F32)

    def cols(h):
        return slice(h * half, (h + 1) * half)

    h = a_states[...].astype(F32)
    mu = jnp.sum(h, axis=1, keepdims=True) * inv
    centred = h - mu
    scale = lax.rsqrt(jnp.sum(centred * centred, axis=1, keepdims=True) * inv + 1e-5)
    normed = centred * scale
    ps, pn, parts = 0.0, 0.0, []
    for k in range(2):
        u = upstream(k, 0)
        n = normed[:, cols(k)]
        p = u * a_gain[:, cols(k)]
        ps = ps + jnp.sum(p, axis=1, keepdims=True)
        pn = pn + jnp.sum(p * n, axis=1, keepdims=True)
        gains[0:1, cols(k)] = jnp.sum(u * n, axis=0, keepdims=True)
        parts.append((p, n))
    for k in range(2):
        p, n = parts[k]
        a_out[:, cols(k)] = (scale * (p - ps * inv - n * (pn * inv))).astype(BF16)

    h = v_states[...].astype(F32)
    scale = lax.rsqrt(jnp.sum(h * h, axis=1, keepdims=True) * inv + 1e-6)
    normed = h * scale
    pn, parts = 0.0, []
    for k in range(2):
        u = upstream(k, 1)
        n = normed[:, cols(k)]
        p = u * v_gain[:, cols(k)]
        pn = pn + jnp.sum(p * n, axis=1, keepdims=True)
        gains[1:2, cols(k)] = jnp.sum(u * n, axis=0, keepdims=True)
        parts.append((p, n))
    for k in range(2):
        p, n = parts[k]
        v_out[:, cols(k)] = (scale * (p - n * (pn * inv))).astype(BF16)


def call(body, outs, specs, scratch=(), out_spec=VM, limit=BIG):
    return pl.pallas_call(
        body,
        out_shape=outs,
        in_specs=specs,
        out_specs=jax.tree.map(lambda _: out_spec, outs),
        scratch_shapes=list(scratch),
        compiler_params=pltpu.CompilerParams(vmem_limit_bytes=limit),
    )


def on_device(
    grad_rows,
    route_ids,
    audio_proj,
    vision_proj,
    audio_states,
    vision_states,
    audio_gain,
    vision_gain,
):
    devices = lax.axis_size("seq")
    lines = devices // 4
    rows, width = grad_rows.shape
    enc, k = audio_proj.shape
    half = enc // 2
    cap = rows // devices
    group = lax.axis_index("groups")
    me = lax.axis_index("seq")
    line, pair, core = me // 4, (me // 2) % 2, me % 2

    block = jax.ShapeDtypeStruct((k, half), BF16)
    if lines == 4:
        keep, to_core, to_pair, to_both = call(
            cut, (block,) * 4, [SM, ANY, ANY], [pltpu.SemaphoreType.DMA((4,))], VM, WHOLE
        )(jnp.stack([pair, core]), audio_proj.T, vision_proj.T)
    else:
        both = jnp.stack([audio_proj.T, vision_proj.T]).reshape(2, k, 2, half)
        pick = lambda m, h: both[m, :, h]
        keep, to_core = pick(core, pair), pick(1 - core, pair)
        to_pair, to_both = pick(core, 1 - pair), pick(1 - core, 1 - pair)
    ids = route_ids[:, 0]
    i_pair = flip(ids, 2, devices)
    i_far = flip(jnp.concatenate([ids, i_pair]), 1, devices)
    all_ids = jnp.concatenate([ids, i_pair, i_far])
    from_core = flip(to_core, 1, devices)
    if lines == 4:
        to_pair, to_both = after((to_pair, to_both), i_pair)
        from_pair = cross(to_pair, 2, devices)
        from_both = cross(to_both, 3, devices)
        straight = core == group
        block1 = jnp.where(straight, keep, from_core)
        mirror1 = jnp.where(straight, from_core, keep)
        f11, b11 = step(block1, block1, 1, devices)
        from_pair, from_both, rows_ready = after((from_pair, from_both, grad_rows), f11, b11)
        rows_ready = after(rows_ready, from_pair, from_both)
        core_ready = after(grad_rows, f11, b11)
    else:
        from_pair = flip(to_pair, 2, devices)
        from_both = flip(to_both, 3, devices)
        rows_ready = core_ready = grad_rows

    r_pair = flip(rows_ready, 2, devices)
    r_core = flip(core_ready, 1, devices)
    low = me % 4
    source = jnp.stack([low, low ^ 2, low ^ 1, low ^ 3])
    named = all_ids // devices == core

    if lines == 4:
        p = jnp.where(group == 0, line, 7 - line)
        straight = core == group
        block1 = jnp.where(straight, keep, from_core)
        mirror1 = jnp.where(straight, from_core, keep)
        spots = jnp.stack([p, pair])
        ends, mids = (0, 3, 4, 7), (1, 2, 5, 6)
        block2 = jnp.where(straight, from_pair, from_both)
        f12, b12 = step(f11, b11, 2, devices)
        f21, b21 = step(block2, block2, 1, devices)
        inner1 = swap(f11, b11, p, mids, devices)
        f22, b22 = step(*after((f21, b21), f12, b12), 2, devices)
        f13, b13 = step(*after((f12, b12), f21, b21), 3, devices)
        inner2 = swap(f21, b21, p, mids, devices)
        mirror2 = cycle(block2, [(a, 7 - a) for a in mids], devices)
        outer1 = swap(f13, b13, p, ends, devices)
        f23, b23 = step(*after((f22, b22), f13, b13), 3, devices)
        r_both = flip(after(r_pair, f23, b23), 1, devices)
        lhs = (grad_rows, r_pair, r_core, r_both)
        outer2 = swap(f23, b23, p, ends, devices)
        chain1 = (block1, mirror1, f11, f12, f13, b11, b12, b13, inner1, outer1)
        chain2 = (block2, mirror2, f21, f22, f23, b21, b22, b23, inner2, outer2)
        base = jnp.where(named, all_ids % devices * cap, -(2 * rows))
        packed = call(
            product_cycle,
            jax.ShapeDtypeStruct((devices, 4, cap, half), BF16),
            [SM, SM] + [VM] * 2 + [ANY] * 24,
            [
                pltpu.VMEM((4 * rows, width), BF16),
                pltpu.VMEM((width, half), BF16),
                pltpu.VMEM((4 * rows, half), F32),
                pltpu.SemaphoreType.DMA((32,)),
            ],
            limit=WHOLE,
        )(spots, source, base[:, None], base[None, :], *chain1, *chain2, *lhs)
        packed = packed.reshape(devices, 4 * cap, half)
    else:
        lhs = (grad_rows, r_pair, r_core, flip(r_pair, 1, devices))
        straight = jnp.stack([keep, from_pair, from_core, from_both])
        plane = jnp.zeros_like(straight).at[source].set(straight)
        ranks = [[a * 4 + w for a in range(lines)] for w in range(4)]
        w = lax.all_gather(plane.reshape(4 * k, half), "seq", axis=0, tiled=True, axis_index_groups=ranks)
        where_from = jnp.repeat(source, rows)
        base = jnp.where(named, (all_ids % devices * 4 + where_from) * cap, -(8 * rows))
        packed = call(product_plain, jax.ShapeDtypeStruct((4 * rows, half), BF16), [VM] * 7)(
            base[:, None], base[None, :], *lhs, w
        )
        packed = packed.reshape(devices, 4 * cap, half)

    arrived = lax.all_to_all(packed, "seq", 0, 0, tiled=True)
    arrived = arrived.reshape(lines, 2, 2, 4, cap, half)
    if cap % 16 != 0:
        arrived = arrived.transpose(1, 2, 0, 3, 4, 5).reshape(1, 2, 2, 1, rows, half)

    audio_grad, vision_grad, gains = call(
        norms,
        (
            jax.ShapeDtypeStruct((rows, enc), BF16),
            jax.ShapeDtypeStruct((rows, enc), BF16),
            jax.ShapeDtypeStruct((2, enc), F32),
        ),
        [VM] * 5,
    )(arrived, audio_states, vision_states, audio_gain[None, :], vision_gain[None, :])
    bit = 1
    while bit < devices:
        near = flip(gains, bit, devices)
        if 2 * bit < devices:
            far = flip(gains, 2 * bit, devices) + flip(gains, 3 * bit, devices)
            gains = (gains + near) + far
        else:
            gains = gains + near
        bit *= 4
    return (audio_grad, vision_grad, gains)


def solution(mesh):
    placed = (
        P(("groups", "seq"), None),
        P(("groups", "seq"), None),
        P(None, "seq"),
        P(None, "seq"),
        P(("groups", "seq"), None),
        P(("groups", "seq"), None),
        P(),
        P(),
    )
    return jax.shard_map(
        on_device,
        mesh=mesh,
        in_specs=placed,
        out_specs=(P(("groups", "seq"), None), P(("groups", "seq"), None), P("groups", None)),
        check_vma=False,
    )
```

```python
import functools

import jax
import jax.numpy as jnp
from jax import lax
from jax.experimental import pallas as pl
from jax.experimental.pallas import tpu as pltpu
from jax.sharding import PartitionSpec as P

F32 = jnp.float32
BF16 = jnp.bfloat16
BOTH = ("groups", "seq")
BIG = 24 * 1024 * 1024
WHOLE = 60 * 1024 * 1024
VM = pl.BlockSpec(memory_space=pltpu.VMEM)
ANY = pl.BlockSpec(memory_space=pl.ANY)


def flip(value, bits, devices):
    return lax.ppermute(value, "seq", [(i, i ^ bits) for i in range(devices)])


def spot(p, low, devices):
    group, line = (0, p) if p < 4 else (1, 7 - p)
    return group * devices + line * 4 + (low ^ group)


def cycle(value, moves, devices):
    pairs = [(spot(a, w, devices), spot(b, w, devices)) for a, b in moves for w in range(4)]
    return lax.ppermute(value, BOTH, pairs)


def after(value, *others):
    return lax.optimization_barrier((value,) + others)[0]


def step(fwd, bwd, k, devices):
    up = [(a, (a + 1) % 8) for a in range(8)]
    down = [(a, (a - 1) % 8) for a in range(8)]
    if k == 3:
        up = [(a, b) for a, b in up if (b - k) % 8 != 7 - b]
        down = [(a, b) for a, b in down if (b + k) % 8 != 7 - b]
    return cycle(fwd, up, devices), cycle(bwd, down, devices)


def swap(fwd, bwd, p, spots, devices):
    first = (p % 4 == 0) | (p % 4 == 1)
    return cycle(jnp.where(first, bwd, fwd), [(a, 7 - a) for a in spots], devices)


def seat():
    me = lax.axis_index("seq")
    return lax.axis_index("groups"), me // 4, lax.rem(me // 2, 2), lax.rem(me, 2)


def cut(a_ref, v_ref, keep, to_pair, to_core, sems):
    group, _, pair, core = seat()
    half = keep.shape[1]
    near = pl.ds(pl.multiple_of(pair * half, 128), half)
    away = pl.ds(pl.multiple_of((1 - pair) * half, 128), half)
    for same in (True, False):
        mine, other = (a_ref, v_ref) if same else (v_ref, a_ref)

        @pl.when((core == group) == same)
        def _():
            pltpu.make_async_copy(mine.at[:, near], keep, sems.at[0]).start()
            pltpu.make_async_copy(mine.at[:, away], to_pair, sems.at[1]).start()
            pltpu.make_async_copy(other.at[:, near], to_core, sems.at[2]).start()

    for i, out in enumerate((keep, to_pair, to_core)):
        pltpu.make_async_copy(a_ref.at[:, near], out, sems.at[i]).wait()


def columns(line, width):
    return pl.ds(pl.multiple_of(line * (width // 4), 128), width // 4)


def line_of(q):
    return jnp.where(q < 4, q, 7 - q)


def load_rows(lhs, lines, buf, sem):
    rows, width = lhs[0].shape
    copies = []
    for j, line in enumerate(lines):
        for s, ref in enumerate(lhs):
            to = buf.at[pl.ds(s * rows, rows), pl.ds(j * (width // 4), width // 4)]
            copies.append(pltpu.make_async_copy(ref.at[:, columns(line, width)], to, sem.at[16 + j * len(lhs) + s]))
    return copies


def second_line(line):
    return jnp.where((line == 0) | (line == 2), 1, 2)


def last_lines(line):
    return jnp.where(line == 0, 2, 0), jnp.where(line == 3, 1, 3)


def product_cycle(*refs):
    ids = refs[:4]
    parts, lhs = refs[4:24], refs[24:28]
    out, buf, w, acc, sems = refs[28:]
    deep = parts[0].shape[0]
    rows = lhs[0].shape[0]
    devices, sources, cap, half = out.shape
    group, line, x, core = seat()
    modality = lax.rem(core + group, 2)
    p = jnp.where(group == 0, line, 7 - line)
    ends = lax.rem(p, 4)
    second = second_line(line)
    third, fourth = last_lines(line)
    copies = load_rows(lhs, (line, second, third, fourth), buf, sems)

    def move(ref, q, slot, which, i):
        start = pl.multiple_of(((slot * 2 + which) * 2 + lax.rem(q // 4 + modality, 2)) * deep, 16)
        return pltpu.make_async_copy(ref, w.at[pl.ds(start, deep)], sems.at[i])

    for j in range(2):
        for c in copies[8 * j : 8 * j + 8]:
            c.start()
        for chain in range(2):
            own, mirror, f1, f2, f3, b1, b2, b3, inner, outer = parts[chain * 10 : chain * 10 + 10]
            which = jnp.where(chain == 0, x, 1 - x)
            f1, f2, f3, b1, b2, b3 = (f1, 7), (f2, 6), (f3, 5), (b1, 1), (b2, 2), (b3, 3)
            inner, outer = (inner, 4), (outer, 4)
            if j == 0:
                move(own, p, 0, which, 4 * chain).start()
            for case in range(4):

                @pl.when(ends == case)
                def _():
                    if j == 0:
                        ref = mirror if chain == 0 else (f1[0], mirror, mirror, b1[0])[case]
                        move(ref, 7 - p, 0, which, 4 * chain + 1).start()
                        takes = ((b1, f2), (b1, inner), (f1, inner), (f1, b2))[case]
                        for i, (ref, step) in enumerate(takes):
                            move(ref, lax.rem(p + step, 8), 1, which, 4 * chain + 2 + i).start()
                    else:
                        takes = ((b2, f3, b3, outer), (f1, f2, b2, b3), (f2, f3, b1, b2), (f2, f3, b3, outer))[case]
                        for i, (ref, step) in enumerate(takes):
                            q = lax.rem(p + step, 8)
                            slot = jnp.where(line_of(q) == third, 2, 3)
                            move(ref, q, slot, which, 8 + 4 * chain + i).start()

    earlier = lax.broadcasted_iota(jnp.int32, (rows, rows), 0) < lax.broadcasted_iota(jnp.int32, (rows, rows), 1)
    earlier = earlier.astype(F32).astype(BF16)
    kinds = lax.broadcasted_iota(jnp.int32, (devices, rows), 0) + modality * devices
    slots = lax.broadcasted_iota(jnp.int32, (devices * cap, rows), 0)
    picks = []
    for id_ref in ids:
        named_by = id_ref[...]
        named = (kinds == named_by).astype(F32)
        before = jnp.dot(named.astype(BF16), earlier, preferred_element_type=F32)
        count = jnp.sum(named * before, axis=0, keepdims=True).astype(jnp.int32)
        slot = (named_by - modality * devices) * cap + count
        picks.append((slots == slot).astype(F32).astype(BF16))
    low = x * 2 + core
    source = (low, (1 - x) * 2 + core, x * 2 + 1 - core, (1 - x) * 2 + 1 - core)
    for j in range(2):
        for c in copies[8 * j : 8 * j + 8]:
            c.wait()
        for i in range(8):
            move(parts[0], p, 0, x, 8 * j + i).wait()
        span = slice(j * 8 * deep, (j + 1) * 8 * deep)
        if j == 0:
            acc[...] = jnp.dot(buf[:, span], w[span, :], preferred_element_type=F32)
    for s in range(4):
        at = slice(s * rows, (s + 1) * rows)
        up = acc[at, :] + jnp.dot(buf[at, span], w[span, :], preferred_element_type=F32)
        packed = jnp.dot(picks[s], up.astype(BF16), preferred_element_type=F32).astype(BF16)
        out[:, source[s]] = packed.reshape(devices, cap, half)


def product_plain(base_col, base_row, l0, l1, l2, l3, w, out):
    rows = l0.shape[0]
    total = 4 * rows
    first = lax.broadcasted_iota(jnp.int32, (total, total), 0)
    second = lax.broadcasted_iota(jnp.int32, (total, total), 1)
    same = jnp.logical_and(base_col[...] == base_row[...], first < second)
    slot = base_row[...] + jnp.sum(same.astype(F32), axis=0, keepdims=True).astype(jnp.int32)
    slots = lax.broadcasted_iota(jnp.int32, (total, rows), 0)
    acc = jnp.zeros(out.shape, F32)
    for s, ref in enumerate((l0, l1, l2, l3)):
        pick = (slots == slot[:, s * rows : (s + 1) * rows]).astype(F32).astype(BF16)
        up = jnp.dot(ref[...], w[...], preferred_element_type=F32).astype(BF16)
        acc = acc + jnp.dot(pick, up, preferred_element_type=F32)
    out[...] = acc.astype(BF16)


def norms(recv, a_states, v_states, a_gain, v_gain, a_out, v_out, gains):
    group = lax.axis_index("groups")
    rows, width = a_states.shape
    half = width // 2
    inv = 1.0 / width

    def upstream(h, m):
        return recv[:, h, lax.rem(m + group, 2)].reshape(rows, half).astype(F32)

    def cols(h):
        return slice(h * half, (h + 1) * half)

    h = a_states[...].astype(F32)
    mu = jnp.sum(h, axis=1, keepdims=True) * inv
    centred = h - mu
    scale = lax.rsqrt(jnp.sum(centred * centred, axis=1, keepdims=True) * inv + 1e-5)
    normed = centred * scale
    ps, pn, parts = 0.0, 0.0, []
    for k in range(2):
        u = upstream(k, 0)
        n = normed[:, cols(k)]
        p = u * a_gain[:, cols(k)]
        ps = ps + jnp.sum(p, axis=1, keepdims=True)
        pn = pn + jnp.sum(p * n, axis=1, keepdims=True)
        gains[0:1, cols(k)] = jnp.sum(u * n, axis=0, keepdims=True)
        parts.append((p, n))
    for k in range(2):
        p, n = parts[k]
        a_out[:, cols(k)] = (scale * (p - ps * inv - n * (pn * inv))).astype(BF16)

    h = v_states[...].astype(F32)
    scale = lax.rsqrt(jnp.sum(h * h, axis=1, keepdims=True) * inv + 1e-6)
    normed = h * scale
    pn, parts = 0.0, []
    for k in range(2):
        u = upstream(k, 1)
        n = normed[:, cols(k)]
        p = u * v_gain[:, cols(k)]
        pn = pn + jnp.sum(p * n, axis=1, keepdims=True)
        gains[1:2, cols(k)] = jnp.sum(u * n, axis=0, keepdims=True)
        parts.append((p, n))
    for k in range(2):
        p, n = parts[k]
        v_out[:, cols(k)] = (scale * (p - n * (pn * inv))).astype(BF16)


def call(body, outs, specs, scratch=(), out_spec=VM, limit=BIG):
    return pl.pallas_call(
        body,
        out_shape=outs,
        in_specs=specs,
        out_specs=jax.tree.map(lambda _: out_spec, outs),
        scratch_shapes=list(scratch),
        compiler_params=pltpu.CompilerParams(vmem_limit_bytes=limit),
    )


def on_device(
    grad_rows,
    route_ids,
    audio_proj,
    vision_proj,
    audio_states,
    vision_states,
    audio_gain,
    vision_gain,
):
    devices = lax.axis_size("seq")
    lines = devices // 4
    rows, width = grad_rows.shape
    enc, k = audio_proj.shape
    half = enc // 2
    cap = rows // devices
    group = lax.axis_index("groups")
    me = lax.axis_index("seq")
    line, pair, core = me // 4, (me // 2) % 2, me % 2

    modality = (core + group) % 2
    ids = route_ids.reshape(1, rows)

    if lines == 4:
        block = jax.ShapeDtypeStruct((k, half), BF16)
        block1, to_pair, to_core = call(
            cut, (block,) * 3, [ANY, ANY], [pltpu.SemaphoreType.DMA((3,))], VM, WHOLE
        )(audio_proj.T, vision_proj.T)
        from_pair = flip(to_pair, 2, devices)
        p = jnp.where(group == 0, line, 7 - line)
        ends, mids = (0, 3, 4, 7), (1, 2, 5, 6)
        f11, b11 = step(block1, block1, 1, devices)
        block2 = after(from_pair, f11, b11)
        r_pair = flip(after(grad_rows, block2), 2, devices)
        r_core = flip(after(grad_rows, block2), 1, devices)
        mirror1 = flip(after(to_core, block2), 1, devices)
        i_core = flip(after(ids, block2), 1, devices)
        inner1 = swap(f11, b11, p, mids, devices)
        f12, b12 = step(f11, b11, 2, devices)
        f21, b21 = step(block2, block2, 1, devices)
        mirror2 = cycle(block2, [(a, 7 - a) for a in mids], devices)
        f22, b22 = step(*after((f21, b21), f12, b12), 2, devices)
        f13, b13 = step(*after((f12, b12), f21, b21, inner1), 3, devices)
        inner2 = swap(f21, b21, p, mids, devices)
        outer1 = swap(f13, b13, p, ends, devices)
        f23, b23 = step(*after((f22, b22), outer1, inner2, mirror2), 3, devices)
        outer2 = swap(f23, b23, p, ends, devices)
        r_there = after(r_pair, f23, b23)
        r_both = flip(r_there, 1, devices)
        late_ids = after(ids, r_there)
        i_pair, i_both = flip(late_ids, 2, devices), flip(late_ids, 3, devices)
        chain1 = (block1, mirror1, f11, f12, f13, b11, b12, b13, inner1, outer1)
        chain2 = (block2, mirror2, f21, f22, f23, b21, b22, b23, inner2, outer2)
        packed = call(
            product_cycle,
            jax.ShapeDtypeStruct((devices, 4, cap, half), BF16),
            [VM] * 4 + [ANY] * 24,
            [
                pltpu.VMEM((4 * rows, width), BF16),
                pltpu.VMEM((width, half), BF16),
                pltpu.VMEM((4 * rows, half), F32),
                pltpu.SemaphoreType.DMA((32,)),
            ],
            limit=WHOLE,
        )(ids, i_pair, i_core, i_both, *chain1, *chain2, grad_rows, r_pair, r_core, r_both)
    else:
        both = jnp.stack([audio_proj.T, vision_proj.T]).reshape(2, k, 2, half)
        plane = [both[modality, :, pair]]
        plane.append(flip(both[modality, :, 1 - pair], 2, devices))
        plane.append(flip(both[1 - modality, :, pair], 1, devices))
        plane.append(flip(both[1 - modality, :, 1 - pair], 3, devices))
        low = me % 4
        source = jnp.stack([low, low ^ 2, low ^ 1, low ^ 3])
        plane = jnp.zeros((4, k, half), BF16).at[source].set(jnp.stack(plane))
        ranks = [[a * 4 + w for a in range(lines)] for w in range(4)]
        w = lax.all_gather(plane.reshape(4 * k, half), "seq", axis=0, tiled=True, axis_index_groups=ranks)
        i_pair = flip(ids, 2, devices)
        i_far = flip(jnp.concatenate([ids, i_pair], axis=1), 1, devices)
        r_pair = flip(grad_rows, 2, devices)
        lhs = (grad_rows, r_pair, flip(grad_rows, 1, devices), flip(r_pair, 1, devices))
        all_ids = jnp.concatenate([ids, i_pair, i_far], axis=1)
        base = (all_ids % devices * 4 + jnp.repeat(source, rows)[None, :]) * cap
        base = jnp.where(all_ids // devices == modality, base, -(8 * rows))
        packed = call(product_plain, jax.ShapeDtypeStruct((4 * rows, half), BF16), [VM] * 7)(
            base.reshape(-1, 1), base, *lhs, w
        )

    packed = packed.reshape(devices, 4 * cap, half)
    arrived = lax.all_to_all(packed, "seq", 0, 0, tiled=True)
    arrived = arrived.reshape(lines, 2, 2, 4, cap, half)
    if cap % 16 != 0:
        arrived = arrived.transpose(1, 2, 0, 3, 4, 5).reshape(1, 2, 2, 1, rows, half)

    audio_grad, vision_grad, gains = call(
        norms,
        (
            jax.ShapeDtypeStruct((rows, enc), BF16),
            jax.ShapeDtypeStruct((rows, enc), BF16),
            jax.ShapeDtypeStruct((2, enc), F32),
        ),
        [VM] * 5,
    )(arrived, audio_states, vision_states, audio_gain[None, :], vision_gain[None, :])
    bit = 1
    while bit < devices:
        gains = gains + flip(gains, bit, devices)
        bit *= 2
    return (audio_grad, vision_grad, gains)


def solution(mesh):
    placed = (
        P(("groups", "seq"), None),
        P(("groups", "seq"), None),
        P(None, "seq"),
        P(None, "seq"),
        P(("groups", "seq"), None),
        P(("groups", "seq"), None),
        P(),
        P(),
    )
    return jax.shard_map(
        on_device,
        mesh=mesh,
        in_specs=placed,
        out_specs=(P(("groups", "seq"), None), P(("groups", "seq"), None), P("groups", None)),
        check_vma=False,
    )
```

```python
import functools

import jax
import jax.numpy as jnp
from jax import lax
from jax.experimental import pallas as pl
from jax.experimental.pallas import tpu as pltpu
from jax.sharding import PartitionSpec as P

F32 = jnp.float32
BF16 = jnp.bfloat16
BOTH = ("groups", "seq")
BIG = 24 * 1024 * 1024
WHOLE = 125 * 512 * 1024
VM = pl.BlockSpec(memory_space=pltpu.VMEM)
ANY = pl.BlockSpec(memory_space=pl.ANY)


def flip(value, bits, devices):
    return lax.ppermute(value, "seq", [(i, i ^ bits) for i in range(devices)])


def spot(p, low, devices):
    group, line = (0, p) if p < 4 else (1, 7 - p)
    return group * devices + line * 4 + (low ^ group)


def cycle(value, moves, devices):
    pairs = [(spot(a, w, devices), spot(b, w, devices)) for a, b in moves for w in range(4)]
    return lax.ppermute(value, BOTH, pairs)


def after(value, *others):
    return lax.optimization_barrier((value,) + others)[0]


def step(fwd, bwd, k, devices):
    up = [(a, (a + 1) % 8) for a in range(8)]
    down = [(a, (a - 1) % 8) for a in range(8)]
    if k == 3:
        up = [(a, b) for a, b in up if (b - k) % 8 != 7 - b]
        down = [(a, b) for a, b in down if (b + k) % 8 != 7 - b]
    return cycle(fwd, up, devices), cycle(bwd, down, devices)


def swap(fwd, bwd, p, spots, devices):
    first = (p % 4 == 0) | (p % 4 == 1)
    return cycle(jnp.where(first, bwd, fwd), [(a, 7 - a) for a in spots], devices)


def seat():
    me = lax.axis_index("seq")
    return lax.axis_index("groups"), me // 4, lax.rem(me // 2, 2), lax.rem(me, 2)


def cut(a_ref, v_ref, keep, to_pair, to_core, sems):
    group, _, pair, core = seat()
    half = keep.shape[1]
    near = pl.ds(pl.multiple_of(pair * half, 128), half)
    away = pl.ds(pl.multiple_of((1 - pair) * half, 128), half)
    for same in (True, False):
        mine, other = (a_ref, v_ref) if same else (v_ref, a_ref)

        @pl.when((core == group) == same)
        def _():
            pltpu.make_async_copy(mine.at[:, near], keep, sems.at[0]).start()
            pltpu.make_async_copy(mine.at[:, away], to_pair, sems.at[1]).start()
            pltpu.make_async_copy(other.at[:, near], to_core, sems.at[2]).start()

    for i, out in enumerate((keep, to_pair, to_core)):
        pltpu.make_async_copy(a_ref.at[:, near], out, sems.at[i]).wait()


def columns(line, width):
    return pl.ds(pl.multiple_of(line * (width // 4), 128), width // 4)


def line_of(q):
    return jnp.where(q < 4, q, 7 - q)


def load_rows(lhs, lines, buf, sem):
    rows, width = lhs[0].shape
    copies = []
    for j, line in enumerate(lines):
        for s, ref in enumerate(lhs):
            to = buf.at[pl.ds(s * rows, rows), pl.ds(j * (width // 4), width // 4)]
            copies.append(pltpu.make_async_copy(ref.at[:, columns(line, width)], to, sem.at[16 + j * len(lhs) + s]))
    return copies


def product_cycle(*refs):
    ids = refs[:4]
    parts, lhs = refs[4:24], refs[24:28]
    out, buf, w, acc, named, sems = refs[28:]
    deep = parts[0].shape[0]
    rows = lhs[0].shape[0]
    devices, sources, cap, half = out.shape
    group, line, x, core = seat()
    modality = lax.rem(core + group, 2)
    p = jnp.where(group == 0, line, 7 - line)
    ends = lax.rem(p, 4)

    def pick(values):
        return jnp.where(ends == 0, values[0], jnp.where(ends == 1, values[1], jnp.where(ends == 2, values[2], values[3])))

    lines = [line_of(lax.rem(p + pick(far), 8)) for far in ((0, 0, 0, 0), (1, 1, 7, 7), (2, 7, 6, 6), (3, 2, 1, 5))]
    row_copies = load_rows(lhs, lines, buf, sems)

    def move(ref, far, slot, chain, i):
        q = lax.rem(p + far, 8)
        which = lax.rem(x + chain, 2)
        start = pl.multiple_of(((slot * 2 + which) * 2 + lax.rem(q // 4 + modality, 2)) * deep, 16)
        return pltpu.make_async_copy(ref, w.at[pl.ds(start, deep)], sems.at[4 * slot + 2 * chain + i])

    def start(slot):
        for c in row_copies[4 * slot : 4 * slot + 4]:
            c.start()
        for chain in range(2):
            own, mirror, f1, f2, f3, b1, b2, b3, inner, outer = parts[chain * 10 : chain * 10 + 10]
            behind = mirror if chain == 0 else f1
            ahead = mirror if chain == 0 else b1
            turn = 7 + 6 * p
            f1, f2, f3, b1, b2, b3 = (f1, 7), (f2, 6), (f3, 5), (b1, 1), (b2, 2), (b3, 3)
            inner, outer, own = (inner, 4), (outer, 4), (own, 0)
            takes = (
                ((own, (behind, turn)), (own, (mirror, turn)), (own, (mirror, turn)), (own, (ahead, turn))),
                ((b1, f2), (b1, inner), (f1, inner), (f1, b2)),
                ((b2, f3), (f1, f2), (f2, f3), (f2, b3)),
                ((b3, outer), (b2, b3), (b1, b2), (f3, outer)),
            )[slot]
            for case in range(4):

                @pl.when(ends == case)
                def _():
                    for i, (ref, far) in enumerate(takes[case]):
                        move(ref, far, slot, chain, i).start()

    def wait(slot):
        for c in row_copies[4 * slot : 4 * slot + 4]:
            c.wait()
        for i in range(4):
            move(parts[0], 0, slot, i // 2, i % 2).wait()

    id_copies = [pltpu.make_async_copy(ref, named.at[s], sems.at[32 + s]) for s, ref in enumerate(ids)]
    for c in id_copies:
        c.start()
    start(0)
    start(1)
    earlier = lax.broadcasted_iota(jnp.int32, (rows, rows), 0) < lax.broadcasted_iota(jnp.int32, (rows, rows), 1)
    earlier = earlier.astype(F32).astype(BF16)
    kinds = lax.broadcasted_iota(jnp.int32, (devices, rows), 0) + modality * devices
    slots = lax.broadcasted_iota(jnp.int32, (devices * cap, rows), 0)
    picks = []
    for c in id_copies:
        c.wait()
    for s in range(4):
        named_by = named[s]
        hit = (kinds == named_by).astype(F32)
        before = jnp.dot(hit.astype(BF16), earlier, preferred_element_type=F32)
        count = jnp.sum(hit * before, axis=0, keepdims=True).astype(jnp.int32)
        slot = (named_by - modality * devices) * cap + count
        picks.append((slots == slot).astype(F32).astype(BF16))
    low = x * 2 + core
    source = (low, (1 - x) * 2 + core, x * 2 + 1 - core, (1 - x) * 2 + 1 - core)
    wait(0)
    wait(1)
    start(2)
    start(3)
    span = slice(0, 8 * deep)
    acc[...] = jnp.dot(buf[:, span], w[span, :], preferred_element_type=F32)
    wait(2)
    wait(3)
    span = slice(8 * deep, 16 * deep)
    for s in range(4):
        at = slice(s * rows, (s + 1) * rows)
        up = acc[at, :] + jnp.dot(buf[at, span], w[span, :], preferred_element_type=F32)
        packed = jnp.dot(picks[s], up.astype(BF16), preferred_element_type=F32).astype(BF16)
        out[:, source[s]] = packed.reshape(devices, cap, half)


def product_plain(base_col, base_row, l0, l1, l2, l3, w, out):
    rows = l0.shape[0]
    total = 4 * rows
    first = lax.broadcasted_iota(jnp.int32, (total, total), 0)
    second = lax.broadcasted_iota(jnp.int32, (total, total), 1)
    same = jnp.logical_and(base_col[...] == base_row[...], first < second)
    slot = base_row[...] + jnp.sum(same.astype(F32), axis=0, keepdims=True).astype(jnp.int32)
    slots = lax.broadcasted_iota(jnp.int32, (total, rows), 0)
    acc = jnp.zeros(out.shape, F32)
    for s, ref in enumerate((l0, l1, l2, l3)):
        pick = (slots == slot[:, s * rows : (s + 1) * rows]).astype(F32).astype(BF16)
        up = jnp.dot(ref[...], w[...], preferred_element_type=F32).astype(BF16)
        acc = acc + jnp.dot(pick, up, preferred_element_type=F32)
    out[...] = acc.astype(BF16)


def statistics(a_states, v_states, a_mean, a_scale, v_scale):
    inv = 1.0 / a_states.shape[1]
    h = a_states[...].astype(F32)
    mean = jnp.sum(h, axis=1, keepdims=True) * inv
    centred = h - mean
    a_mean[...] = mean
    a_scale[...] = lax.rsqrt(jnp.sum(centred * centred, axis=1, keepdims=True) * inv + 1e-5)
    g = v_states[...].astype(F32)
    v_scale[...] = lax.rsqrt(jnp.sum(g * g, axis=1, keepdims=True) * inv + 1e-6)


def upstream(recv, h, m, rows):
    column = lax.rem(m + lax.axis_index("groups"), 2)
    return recv[:, h, column].reshape(rows, recv.shape[-1]).astype(F32)


def gain_sums(recv, a_states, v_states, a_mean, a_scale, v_scale, gains):
    rows, width = a_states.shape
    half = width // 2
    sides = ((a_states, a_mean[...], a_scale), (v_states, 0.0, v_scale))
    for m, (states, mean, scale) in enumerate(sides):
        for h in range(2):
            cols = slice(h * half, (h + 1) * half)
            n = (states[:, cols].astype(F32) - mean) * scale[...]
            gains[m : m + 1, cols] = jnp.sum(upstream(recv, h, m, rows) * n, axis=0, keepdims=True)


def norms(recv, a_states, v_states, a_mean, a_scale, v_scale, a_gain, v_gain, a_out, v_out):
    rows, width = a_states.shape
    half = width // 2
    inv = 1.0 / width
    sides = ((a_states, a_mean[...], a_scale, a_gain, a_out), (v_states, 0.0, v_scale, v_gain, v_out))
    for m, (states, mean, scale, gain, out) in enumerate(sides):
        ps, pn, parts = 0.0, 0.0, []
        for h in range(2):
            cols = slice(h * half, (h + 1) * half)
            n = (states[:, cols].astype(F32) - mean) * scale[...]
            p = upstream(recv, h, m, rows) * gain[:, cols]
            ps = ps + jnp.sum(p, axis=1, keepdims=True)
            pn = pn + jnp.sum(p * n, axis=1, keepdims=True)
            parts.append((p, n, cols))
        for p, n, cols in parts:
            if m == 0:
                p = p - ps * inv
            out[:, cols] = (scale[...] * (p - n * (pn * inv))).astype(BF16)


def call(body, outs, specs, scratch=(), out_spec=VM, limit=BIG):
    return pl.pallas_call(
        body,
        out_shape=outs,
        in_specs=specs,
        out_specs=jax.tree.map(lambda _: out_spec, outs),
        scratch_shapes=list(scratch),
        compiler_params=pltpu.CompilerParams(vmem_limit_bytes=limit),
    )


def on_device(
    grad_rows,
    route_ids,
    audio_proj,
    vision_proj,
    audio_states,
    vision_states,
    audio_gain,
    vision_gain,
):
    devices = lax.axis_size("seq")
    lines = devices // 4
    rows, width = grad_rows.shape
    enc, k = audio_proj.shape
    half = enc // 2
    cap = rows // devices
    group = lax.axis_index("groups")
    me = lax.axis_index("seq")
    line, pair, core = me // 4, (me // 2) % 2, me % 2

    modality = (core + group) % 2
    ids = route_ids.reshape(1, rows)

    if lines == 4:
        block = jax.ShapeDtypeStruct((k, half), BF16)
        block1, to_pair, to_core = call(
            cut, (block,) * 3, [ANY, ANY], [pltpu.SemaphoreType.DMA((3,))], VM, WHOLE
        )(audio_proj.T, vision_proj.T)
        from_pair = flip(to_pair, 2, devices)
        p = jnp.where(group == 0, line, 7 - line)
        ends, mids = (0, 3, 4, 7), (1, 2, 5, 6)
        f11, b11 = step(block1, block1, 1, devices)
        block2 = after(from_pair, f11, b11)
        r_pair = flip(after(grad_rows, block2), 2, devices)
        r_core = flip(after(grad_rows, block2), 1, devices)
        mirror1 = flip(after(to_core, block2), 1, devices)
        i_core = flip(after(ids, block2), 1, devices)
        inner1 = swap(f11, b11, p, mids, devices)
        f12, b12 = step(f11, b11, 2, devices)
        f21, b21 = step(block2, block2, 1, devices)
        mirror2 = cycle(block2, [(a, 7 - a) for a in mids], devices)
        f22, b22 = step(*after((f21, b21), f12, b12), 2, devices)
        f13, b13 = step(*after((f12, b12), f21, b21, inner1), 3, devices)
        inner2 = swap(f21, b21, p, mids, devices)
        outer1 = swap(f13, b13, p, ends, devices)
        f23, b23 = step(*after((f22, b22), outer1, inner2, mirror2), 3, devices)
        outer2 = swap(f23, b23, p, ends, devices)
        r_there = after(r_pair, f23, b23)
        r_both = flip(r_there, 1, devices)
        late_ids = after(ids, r_there)
        i_pair, i_both = flip(late_ids, 2, devices), flip(late_ids, 3, devices)
        chain1 = (block1, mirror1, f11, f12, f13, b11, b12, b13, inner1, outer1)
        chain2 = (block2, mirror2, f21, f22, f23, b21, b22, b23, inner2, outer2)
        packed = call(
            product_cycle,
            jax.ShapeDtypeStruct((devices, 4, cap, half), BF16),
            [ANY] * 28,
            [
                pltpu.VMEM((4 * rows, width), BF16),
                pltpu.VMEM((width, half), BF16),
                pltpu.VMEM((4 * rows, half), F32),
                pltpu.VMEM((4, 1, rows), jnp.int32),
                pltpu.SemaphoreType.DMA((36,)),
            ],
            limit=WHOLE,
        )(ids, i_pair, i_core, i_both, *chain1, *chain2, grad_rows, r_pair, r_core, r_both)
    else:
        both = jnp.stack([audio_proj.T, vision_proj.T]).reshape(2, k, 2, half)
        plane = [both[modality, :, pair]]
        plane.append(flip(both[modality, :, 1 - pair], 2, devices))
        plane.append(flip(both[1 - modality, :, pair], 1, devices))
        plane.append(flip(both[1 - modality, :, 1 - pair], 3, devices))
        low = me % 4
        source = jnp.stack([low, low ^ 2, low ^ 1, low ^ 3])
        plane = jnp.zeros((4, k, half), BF16).at[source].set(jnp.stack(plane))
        ranks = [[a * 4 + w for a in range(lines)] for w in range(4)]
        w = lax.all_gather(plane.reshape(4 * k, half), "seq", axis=0, tiled=True, axis_index_groups=ranks)
        i_pair = flip(ids, 2, devices)
        i_far = flip(jnp.concatenate([ids, i_pair], axis=1), 1, devices)
        r_pair = flip(grad_rows, 2, devices)
        lhs = (grad_rows, r_pair, flip(grad_rows, 1, devices), flip(r_pair, 1, devices))
        all_ids = jnp.concatenate([ids, i_pair, i_far], axis=1)
        base = (all_ids % devices * 4 + jnp.repeat(source, rows)[None, :]) * cap
        base = jnp.where(all_ids // devices == modality, base, -(8 * rows))
        packed = call(product_plain, jax.ShapeDtypeStruct((4 * rows, half), BF16), [VM] * 7)(
            base.reshape(-1, 1), base, *lhs, w
        )

    packed = packed.reshape(devices, 4 * cap, half)
    arrived = lax.all_to_all(packed, "seq", 0, 0, tiled=True)
    arrived = arrived.reshape(lines, 2, 2, 4, cap, half)
    if cap % 16 != 0:
        arrived = arrived.transpose(1, 2, 0, 3, 4, 5).reshape(1, 2, 2, 1, rows, half)

    thin = jax.ShapeDtypeStruct((rows, 1), F32)
    states = (audio_states, vision_states)
    states += tuple(call(statistics, (thin,) * 3, [VM] * 2)(*states))
    gains = call(gain_sums, jax.ShapeDtypeStruct((2, enc), F32), [VM] * 6)(arrived, *states)
    grad = jax.ShapeDtypeStruct((rows, enc), BF16)
    audio_grad, vision_grad = call(norms, (grad, grad), [VM] * 8)(
        arrived, *states, audio_gain[None, :], vision_gain[None, :]
    )
    bit = 1
    while bit < devices:
        gains = gains + flip(gains, bit, devices)
        bit *= 2
    return (audio_grad, vision_grad, gains)


def solution(mesh):
    placed = (
        P(("groups", "seq"), None),
        P(("groups", "seq"), None),
        P(None, "seq"),
        P(None, "seq"),
        P(("groups", "seq"), None),
        P(("groups", "seq"), None),
        P(),
        P(),
    )
    return jax.shard_map(
        on_device,
        mesh=mesh,
        in_specs=placed,
        out_specs=(P(("groups", "seq"), None), P(("groups", "seq"), None), P("groups", None)),
        check_vma=False,
    )
```

```python
import functools

import jax
import jax.numpy as jnp
from jax import lax
from jax.experimental import pallas as pl
from jax.experimental.pallas import tpu as pltpu
from jax.sharding import PartitionSpec as P

F32 = jnp.float32
BF16 = jnp.bfloat16
BOTH = ("groups", "seq")
BIG = 24 * 1024 * 1024
WHOLE = 125 * 512 * 1024
VM = pl.BlockSpec(memory_space=pltpu.VMEM)
ANY = pl.BlockSpec(memory_space=pl.ANY)


def flip(value, bits, devices):
    return lax.ppermute(value, "seq", [(i, i ^ bits) for i in range(devices)])


def spot(p, low, devices):
    group, line = (0, p) if p < 4 else (1, 7 - p)
    return group * devices + line * 4 + (low ^ group)


def cycle(value, moves, devices):
    pairs = [(spot(a, w, devices), spot(b, w, devices)) for a, b in moves for w in range(4)]
    return lax.ppermute(value, BOTH, pairs)


def after(value, *others):
    return lax.optimization_barrier((value,) + others)[0]


def step(fwd, bwd, k, devices):
    up = [(a, (a + 1) % 8) for a in range(8)]
    down = [(a, (a - 1) % 8) for a in range(8)]
    if k == 3:
        up = [(a, b) for a, b in up if (b - k) % 8 != 7 - b]
        down = [(a, b) for a, b in down if (b + k) % 8 != 7 - b]
    return cycle(fwd, up, devices), cycle(bwd, down, devices)


def swap(fwd, bwd, p, spots, devices):
    first = (p % 4 == 0) | (p % 4 == 1)
    return cycle(jnp.where(first, bwd, fwd), [(a, 7 - a) for a in spots], devices)


def seat():
    me = lax.axis_index("seq")
    return lax.axis_index("groups"), me // 4, lax.rem(me // 2, 2), lax.rem(me, 2)


def cut(a_ref, v_ref, keep, to_pair, sems):
    group, _, pair, core = seat()
    half = keep.shape[1]
    near = pl.ds(pl.multiple_of(pair * half, 128), half)
    away = pl.ds(pl.multiple_of((1 - pair) * half, 128), half)
    for same in (True, False):
        mine = a_ref if same else v_ref

        @pl.when((core == group) == same)
        def _():
            pltpu.make_async_copy(mine.at[:, near], keep, sems.at[0]).start()
            pltpu.make_async_copy(mine.at[:, away], to_pair, sems.at[1]).start()

    for i, out in enumerate((keep, to_pair)):
        pltpu.make_async_copy(a_ref.at[:, near], out, sems.at[i]).wait()


def columns(line, width):
    return pl.ds(pl.multiple_of(line * (width // 4), 128), width // 4)


def line_of(q):
    return jnp.where(q < 4, q, 7 - q)


def load_rows(lhs, lines, buf, sem):
    rows, width = lhs[0].shape
    copies = []
    for j, line in enumerate(lines):
        for s, ref in enumerate(lhs):
            to = buf.at[pl.ds(s * rows, rows), pl.ds(j * (width // 4), width // 4)]
            copies.append(pltpu.make_async_copy(ref.at[:, columns(line, width)], to, sem.at[16 + j * len(lhs) + s]))
    return copies


def product_cycle(*refs):
    ids = refs[:4]
    parts, lhs = refs[4:15], refs[15:19]
    out, buf, w, acc, named, sems = refs[19:]
    deep = parts[0].shape[0] // 2
    rows = lhs[0].shape[0]
    devices, sources, cap, half = out.shape
    group, line, x, core = seat()
    modality = lax.rem(core + group, 2)
    p = jnp.where(group == 0, line, 7 - line)
    ends = lax.rem(p, 4)

    def pick(values):
        return jnp.where(ends == 0, values[0], jnp.where(ends == 1, values[1], jnp.where(ends == 2, values[2], values[3])))

    lines = [line_of(lax.rem(p + pick(far), 8)) for far in ((0, 0, 0, 0), (1, 1, 7, 7), (2, 7, 6, 6), (3, 2, 1, 5))]
    row_copies = load_rows(lhs, lines, buf, sems)

    def move(ref, far, slot, i):
        core_of = lax.rem(lax.rem(p + far, 8) // 4 + modality, 2)
        out = []
        for part in range(2):
            place = (slot * 2 + lax.rem(x + part, 2)) * 2 + core_of
            to = w.at[pl.ds(pl.multiple_of(place * deep, 16), deep)]
            src = ref[part] if isinstance(ref, tuple) else ref.at[pl.ds(part * deep, deep)]
            out.append(pltpu.make_async_copy(src, to, sems.at[4 * slot + 2 * i + part]))
        return out

    def start(slot):
        for c in row_copies[4 * slot : 4 * slot + 4]:
            c.start()
        own, mirror, f1, f2, f3, b1, b2, b3, inner = parts[:9]
        outer = (parts[9], parts[10])
        turn = 7 + 6 * p
        behind, ahead = (f1, turn), (b1, turn)
        f1, f2, f3, b1, b2, b3 = (f1, 7), (f2, 6), (f3, 5), (b1, 1), (b2, 2), (b3, 3)
        inner, outer, own, mirror = (inner, 4), (outer, 4), (own, 0), (mirror, turn)
        takes = (
            ((own, behind), (own, mirror), (own, mirror), (own, ahead)),
            ((b1, f2), (b1, inner), (f1, inner), (f1, b2)),
            ((b2, f3), (f1, f2), (f2, f3), (f2, b3)),
            ((b3, outer), (b2, b3), (b1, b2), (f3, outer)),
        )[slot]
        for case in range(4):

            @pl.when(ends == case)
            def _():
                for i, (ref, far) in enumerate(takes[case]):
                    for c in move(ref, far, slot, i):
                        c.start()

    def wait(slot):
        for c in row_copies[4 * slot : 4 * slot + 4]:
            c.wait()
        for i in range(2):
            for c in move(parts[0], 0, slot, i):
                c.wait()

    id_copies = [pltpu.make_async_copy(ref, named.at[s], sems.at[32 + s]) for s, ref in enumerate(ids)]
    for c in id_copies:
        c.start()
    start(0)
    start(1)
    earlier = lax.broadcasted_iota(jnp.int32, (rows, rows), 0) < lax.broadcasted_iota(jnp.int32, (rows, rows), 1)
    earlier = earlier.astype(F32).astype(BF16)
    kinds = lax.broadcasted_iota(jnp.int32, (devices, rows), 0) + modality * devices
    slots = lax.broadcasted_iota(jnp.int32, (devices * cap, rows), 0)
    picks = []
    for c in id_copies:
        c.wait()
    for s in range(4):
        named_by = named[s]
        hit = (kinds == named_by).astype(F32)
        before = jnp.dot(hit.astype(BF16), earlier, preferred_element_type=F32)
        count = jnp.sum(hit * before, axis=0, keepdims=True).astype(jnp.int32)
        slot = (named_by - modality * devices) * cap + count
        picks.append((slots == slot).astype(F32).astype(BF16))
    low = x * 2 + core
    source = (low, (1 - x) * 2 + core, x * 2 + 1 - core, (1 - x) * 2 + 1 - core)
    wait(0)
    wait(1)
    start(2)
    start(3)
    span = slice(0, 8 * deep)
    acc[...] = jnp.dot(buf[:, span], w[span, :], preferred_element_type=F32)
    wait(2)
    wait(3)
    span = slice(8 * deep, 16 * deep)
    for s in range(4):
        at = slice(s * rows, (s + 1) * rows)
        up = acc[at, :] + jnp.dot(buf[at, span], w[span, :], preferred_element_type=F32)
        packed = jnp.dot(picks[s], up.astype(BF16), preferred_element_type=F32).astype(BF16)
        out[:, source[s]] = packed.reshape(devices, cap, half)


def product_plain(base_col, base_row, l0, l1, l2, l3, w, out):
    rows = l0.shape[0]
    total = 4 * rows
    first = lax.broadcasted_iota(jnp.int32, (total, total), 0)
    second = lax.broadcasted_iota(jnp.int32, (total, total), 1)
    same = jnp.logical_and(base_col[...] == base_row[...], first < second)
    slot = base_row[...] + jnp.sum(same.astype(F32), axis=0, keepdims=True).astype(jnp.int32)
    slots = lax.broadcasted_iota(jnp.int32, (total, rows), 0)
    acc = jnp.zeros(out.shape, F32)
    for s, ref in enumerate((l0, l1, l2, l3)):
        pick = (slots == slot[:, s * rows : (s + 1) * rows]).astype(F32).astype(BF16)
        up = jnp.dot(ref[...], w[...], preferred_element_type=F32).astype(BF16)
        acc = acc + jnp.dot(pick, up, preferred_element_type=F32)
    out[...] = acc.astype(BF16)


def statistics(a_states, v_states, a_mean, a_scale, v_scale):
    inv = 1.0 / a_states.shape[1]
    h = a_states[...].astype(F32)
    mean = jnp.sum(h, axis=1, keepdims=True) * inv
    centred = h - mean
    a_mean[...] = mean
    a_scale[...] = lax.rsqrt(jnp.sum(centred * centred, axis=1, keepdims=True) * inv + 1e-5)
    g = v_states[...].astype(F32)
    v_scale[...] = lax.rsqrt(jnp.sum(g * g, axis=1, keepdims=True) * inv + 1e-6)


def upstream(recv, h, m, rows):
    column = lax.rem(m + lax.axis_index("groups"), 2)
    return recv[:, h, column].reshape(rows, recv.shape[-1]).astype(F32)


def gain_sums(recv, a_states, v_states, a_mean, a_scale, v_scale, gains):
    rows, width = a_states.shape
    half = width // 2
    sides = ((a_states, a_mean[...], a_scale), (v_states, 0.0, v_scale))
    for m, (states, mean, scale) in enumerate(sides):
        for h in range(2):
            cols = slice(h * half, (h + 1) * half)
            n = (states[:, cols].astype(F32) - mean) * scale[...]
            gains[m : m + 1, cols] = jnp.sum(upstream(recv, h, m, rows) * n, axis=0, keepdims=True)


def norms(recv, a_states, v_states, a_mean, a_scale, v_scale, a_gain, v_gain, a_out, v_out):
    rows, width = a_states.shape
    half = width // 2
    inv = 1.0 / width
    sides = ((a_states, a_mean[...], a_scale, a_gain, a_out), (v_states, 0.0, v_scale, v_gain, v_out))
    for m, (states, mean, scale, gain, out) in enumerate(sides):
        ps, pn, parts = 0.0, 0.0, []
        for h in range(2):
            cols = slice(h * half, (h + 1) * half)
            n = (states[:, cols].astype(F32) - mean) * scale[...]
            p = upstream(recv, h, m, rows) * gain[:, cols]
            ps = ps + jnp.sum(p, axis=1, keepdims=True)
            pn = pn + jnp.sum(p * n, axis=1, keepdims=True)
            parts.append((p, n, cols))
        for p, n, cols in parts:
            if m == 0:
                p = p - ps * inv
            out[:, cols] = (scale[...] * (p - n * (pn * inv))).astype(BF16)


def call(body, outs, specs, scratch=(), out_spec=VM, limit=BIG):
    return pl.pallas_call(
        body,
        out_shape=outs,
        in_specs=specs,
        out_specs=jax.tree.map(lambda _: out_spec, outs),
        scratch_shapes=list(scratch),
        compiler_params=pltpu.CompilerParams(vmem_limit_bytes=limit),
    )


def on_device(
    grad_rows,
    route_ids,
    audio_proj,
    vision_proj,
    audio_states,
    vision_states,
    audio_gain,
    vision_gain,
):
    devices = lax.axis_size("seq")
    lines = devices // 4
    rows, width = grad_rows.shape
    enc, k = audio_proj.shape
    half = enc // 2
    cap = rows // devices
    group = lax.axis_index("groups")
    me = lax.axis_index("seq")
    line, pair, core = me // 4, (me // 2) % 2, me % 2

    modality = (core + group) % 2
    ids = route_ids.reshape(1, rows)

    if lines == 4:
        block = jax.ShapeDtypeStruct((k, half), BF16)
        keep, to_pair = call(cut, (block,) * 2, [ANY, ANY], [pltpu.SemaphoreType.DMA((2,))], VM, WHOLE)(
            audio_proj.T, vision_proj.T
        )
        from_pair = flip(to_pair, 2, devices)
        whole = jnp.concatenate([keep, from_pair])
        r_pair = flip(after(grad_rows, from_pair), 2, devices)
        p = jnp.where(group == 0, line, 7 - line)
        ends, mids = (0, 3, 4, 7), (1, 2, 5, 6)
        f1, b1 = step(whole, whole, 1, devices)
        r_core = flip(after(grad_rows, f1, b1), 1, devices)
        i_core = flip(after(ids, f1, b1), 1, devices)
        mirror = cycle(whole, [(a, 7 - a) for a in mids], devices)
        f2, b2 = step(f1, b1, 2, devices)
        inner = swap(f1, b1, p, mids, devices)
        f3, b3 = step(*after((f2, b2), inner, mirror), 3, devices)
        opposite = jnp.where(p % 4 < 2, b3, f3)
        over_y = cycle(opposite[:k], [(a, 7 - a) for a in ends], devices)
        along_z = cycle(opposite[k:], [(1, 0), (2, 3), (5, 4), (6, 7)], devices)
        r_there = after(r_pair, f3, b3)
        r_both = flip(r_there, 1, devices)
        late_ids = after(ids, r_there)
        i_pair, i_both = flip(late_ids, 2, devices), flip(late_ids, 3, devices)
        chain = (whole, mirror, f1, f2, f3, b1, b2, b3, inner, over_y, along_z)
        packed = call(
            product_cycle,
            jax.ShapeDtypeStruct((devices, 4, cap, half), BF16),
            [ANY] * 19,
            [
                pltpu.VMEM((4 * rows, width), BF16),
                pltpu.VMEM((width, half), BF16),
                pltpu.VMEM((4 * rows, half), F32),
                pltpu.VMEM((4, 1, rows), jnp.int32),
                pltpu.SemaphoreType.DMA((36,)),
            ],
            limit=WHOLE,
        )(ids, i_pair, i_core, i_both, *chain, grad_rows, r_pair, r_core, r_both)
    else:
        both = jnp.stack([audio_proj.T, vision_proj.T]).reshape(2, k, 2, half)
        plane = [both[modality, :, pair]]
        plane.append(flip(both[modality, :, 1 - pair], 2, devices))
        plane.append(flip(both[1 - modality, :, pair], 1, devices))
        plane.append(flip(both[1 - modality, :, 1 - pair], 3, devices))
        low = me % 4
        source = jnp.stack([low, low ^ 2, low ^ 1, low ^ 3])
        plane = jnp.zeros((4, k, half), BF16).at[source].set(jnp.stack(plane))
        ranks = [[a * 4 + w for a in range(lines)] for w in range(4)]
        w = lax.all_gather(plane.reshape(4 * k, half), "seq", axis=0, tiled=True, axis_index_groups=ranks)
        i_pair = flip(ids, 2, devices)
        i_far = flip(jnp.concatenate([ids, i_pair], axis=1), 1, devices)
        r_pair = flip(grad_rows, 2, devices)
        lhs = (grad_rows, r_pair, flip(grad_rows, 1, devices), flip(r_pair, 1, devices))
        all_ids = jnp.concatenate([ids, i_pair, i_far], axis=1)
        base = (all_ids % devices * 4 + jnp.repeat(source, rows)[None, :]) * cap
        base = jnp.where(all_ids // devices == modality, base, -(8 * rows))
        packed = call(product_plain, jax.ShapeDtypeStruct((4 * rows, half), BF16), [VM] * 7)(
            base.reshape(-1, 1), base, *lhs, w
        )

    packed = packed.reshape(devices, 4 * cap, half)
    arrived = lax.all_to_all(packed, "seq", 0, 0, tiled=True)
    arrived = arrived.reshape(lines, 2, 2, 4, cap, half)
    if cap % 16 != 0:
        arrived = arrived.transpose(1, 2, 0, 3, 4, 5).reshape(1, 2, 2, 1, rows, half)

    thin = jax.ShapeDtypeStruct((rows, 1), F32)
    states = (audio_states, vision_states)
    states += tuple(call(statistics, (thin,) * 3, [VM] * 2)(*states))
    gains = call(gain_sums, jax.ShapeDtypeStruct((2, enc), F32), [VM] * 6)(arrived, *states)
    grad = jax.ShapeDtypeStruct((rows, enc), BF16)
    audio_grad, vision_grad = call(norms, (grad, grad), [VM] * 8)(
        arrived, *states, audio_gain[None, :], vision_gain[None, :]
    )
    bit = 1
    while bit < devices:
        gains = gains + flip(gains, bit, devices)
        bit *= 2
    return (audio_grad, vision_grad, gains)


def solution(mesh):
    placed = (
        P(("groups", "seq"), None),
        P(("groups", "seq"), None),
        P(None, "seq"),
        P(None, "seq"),
        P(("groups", "seq"), None),
        P(("groups", "seq"), None),
        P(),
        P(),
    )
    return jax.shard_map(
        on_device,
        mesh=mesh,
        in_specs=placed,
        out_specs=(P(("groups", "seq"), None), P(("groups", "seq"), None), P("groups", None)),
        check_vma=False,
    )
```

```python
import functools

import jax
import jax.numpy as jnp
from jax import lax
from jax.experimental import pallas as pl
from jax.experimental.pallas import tpu as pltpu
from jax.sharding import PartitionSpec as P

F32 = jnp.float32
BF16 = jnp.bfloat16
BOTH = ("groups", "seq")
BIG = 24 * 1024 * 1024
WHOLE = 125 * 512 * 1024
VM = pl.BlockSpec(memory_space=pltpu.VMEM)
ANY = pl.BlockSpec(memory_space=pl.ANY)


def flip(value, bits, devices):
    return lax.ppermute(value, "seq", [(i, i ^ bits) for i in range(devices)])


def spot(p, low, devices):
    group, line = (0, p) if p < 4 else (1, 7 - p)
    return group * devices + line * 4 + (low ^ group)


def cycle(value, moves, devices):
    pairs = [(spot(a, w, devices), spot(b, w, devices)) for a, b in moves for w in range(4)]
    return lax.ppermute(value, BOTH, pairs)


def after(value, *others):
    return lax.optimization_barrier((value,) + others)[0]


def step(fwd, bwd, k, devices):
    up = [(a, (a + 1) % 8) for a in range(8)]
    down = [(a, (a - 1) % 8) for a in range(8)]
    if k == 3:
        up = [(a, b) for a, b in up if (b - k) % 8 != 7 - b]
        down = [(a, b) for a, b in down if (b + k) % 8 != 7 - b]
    return cycle(fwd, up, devices), cycle(bwd, down, devices)


def swap(fwd, bwd, p, spots, devices):
    first = (p % 4 == 0) | (p % 4 == 1)
    return cycle(jnp.where(first, bwd, fwd), [(a, 7 - a) for a in spots], devices)


def seat():
    me = lax.axis_index("seq")
    return lax.axis_index("groups"), me // 4, lax.rem(me // 2, 2), lax.rem(me, 2)


def cut(a_ref, v_ref, keep, to_pair, sems):
    group, _, pair, core = seat()
    half = keep.shape[1]
    near = pl.ds(pl.multiple_of(pair * half, 128), half)
    away = pl.ds(pl.multiple_of((1 - pair) * half, 128), half)
    for same in (True, False):
        mine = a_ref if same else v_ref

        @pl.when((core == group) == same)
        def _():
            pltpu.make_async_copy(mine.at[:, near], keep, sems.at[0]).start()
            pltpu.make_async_copy(mine.at[:, away], to_pair, sems.at[1]).start()

    for i, out in enumerate((keep, to_pair)):
        pltpu.make_async_copy(a_ref.at[:, near], out, sems.at[i]).wait()


def columns(line, width):
    return pl.ds(pl.multiple_of(line * (width // 4), 128), width // 4)


def line_of(q):
    return jnp.where(q < 4, q, 7 - q)


def load_rows(lhs, lines, buf, sem):
    rows, width = lhs[0].shape
    copies = []
    for j, line in enumerate(lines):
        for s, ref in enumerate(lhs):
            to = buf.at[pl.ds(s * rows, rows), pl.ds(j * (width // 4), width // 4)]
            copies.append(pltpu.make_async_copy(ref.at[:, columns(line, width)], to, sem.at[16 + j * len(lhs) + s]))
    return copies


def product_cycle(*refs):
    ids = refs[:4]
    parts, lhs = refs[4:15], refs[15:19]
    out, buf, w, acc, named, sems = refs[19:]
    deep = parts[0].shape[0] // 2
    rows = lhs[0].shape[0]
    devices, sources, cap, half = out.shape
    group, line, x, core = seat()
    modality = lax.rem(core + group, 2)
    p = jnp.where(group == 0, line, 7 - line)
    ends = lax.rem(p, 4)

    def pick(values):
        return jnp.where(ends == 0, values[0], jnp.where(ends == 1, values[1], jnp.where(ends == 2, values[2], values[3])))

    lines = [line_of(lax.rem(p + pick(far), 8)) for far in ((0, 0, 0, 0), (1, 1, 7, 7), (2, 7, 6, 6), (3, 2, 1, 5))]
    row_copies = load_rows(lhs, lines, buf, sems)

    def move(ref, far, slot, i):
        core_of = lax.rem(lax.rem(p + far, 8) // 4 + modality, 2)
        out = []
        for part in range(2):
            place = (slot * 2 + lax.rem(x + part, 2)) * 2 + core_of
            to = w.at[pl.ds(pl.multiple_of(place * deep, 16), deep)]
            src = ref[part] if isinstance(ref, tuple) else ref.at[pl.ds(part * deep, deep)]
            out.append(pltpu.make_async_copy(src, to, sems.at[4 * slot + 2 * i + part]))
        return out

    def start(slot):
        for c in row_copies[4 * slot : 4 * slot + 4]:
            c.start()
        own, mirror, f1, f2, f3, b1, b2, b3, inner = parts[:9]
        outer = (parts[9], parts[10])
        turn = 7 + 6 * p
        behind, ahead = (f1, turn), (b1, turn)
        f1, f2, f3, b1, b2, b3 = (f1, 7), (f2, 6), (f3, 5), (b1, 1), (b2, 2), (b3, 3)
        inner, outer, own, mirror = (inner, 4), (outer, 4), (own, 0), (mirror, turn)
        takes = (
            ((own, behind), (own, mirror), (own, mirror), (own, ahead)),
            ((b1, f2), (b1, inner), (f1, inner), (f1, b2)),
            ((b2, f3), (f1, f2), (f2, f3), (f2, b3)),
            ((b3, outer), (b2, b3), (b1, b2), (f3, outer)),
        )[slot]
        for case in range(4):

            @pl.when(ends == case)
            def _():
                for i, (ref, far) in enumerate(takes[case]):
                    for c in move(ref, far, slot, i):
                        c.start()

    def wait(slot):
        for c in row_copies[4 * slot : 4 * slot + 4]:
            c.wait()
        for i in range(2):
            for c in move(parts[0], 0, slot, i):
                c.wait()

    id_copies = [pltpu.make_async_copy(ref, named.at[s], sems.at[32 + s]) for s, ref in enumerate(ids)]
    for c in id_copies:
        c.start()
    start(0)
    start(1)
    earlier = lax.broadcasted_iota(jnp.int32, (rows, rows), 0) < lax.broadcasted_iota(jnp.int32, (rows, rows), 1)
    earlier = earlier.astype(F32).astype(BF16)
    kinds = lax.broadcasted_iota(jnp.int32, (devices, rows), 0) + modality * devices
    slots = lax.broadcasted_iota(jnp.int32, (devices * cap, rows), 0)
    picks = []
    for c in id_copies:
        c.wait()
    for s in range(4):
        named_by = named[s]
        hit = (kinds == named_by).astype(F32)
        before = jnp.dot(hit.astype(BF16), earlier, preferred_element_type=F32)
        count = jnp.sum(hit * before, axis=0, keepdims=True).astype(jnp.int32)
        slot = (named_by - modality * devices) * cap + count
        picks.append((slots == slot).astype(F32).astype(BF16))
    low = x * 2 + core
    source = (low, (1 - x) * 2 + core, x * 2 + 1 - core, (1 - x) * 2 + 1 - core)
    wait(0)
    wait(1)
    start(2)
    start(3)
    span = slice(0, 8 * deep)
    acc[...] = jnp.dot(buf[:, span], w[span, :], preferred_element_type=F32)
    wait(2)
    wait(3)
    span = slice(8 * deep, 16 * deep)
    for s in range(4):
        at = slice(s * rows, (s + 1) * rows)
        up = acc[at, :] + jnp.dot(buf[at, span], w[span, :], preferred_element_type=F32)
        packed = jnp.dot(picks[s], up.astype(BF16), preferred_element_type=F32).astype(BF16)
        out[:, source[s]] = packed.reshape(devices, cap, half)


def product_plain(base_col, base_row, l0, l1, l2, l3, w, out):
    rows = l0.shape[0]
    total = 4 * rows
    first = lax.broadcasted_iota(jnp.int32, (total, total), 0)
    second = lax.broadcasted_iota(jnp.int32, (total, total), 1)
    same = jnp.logical_and(base_col[...] == base_row[...], first < second)
    slot = base_row[...] + jnp.sum(same.astype(F32), axis=0, keepdims=True).astype(jnp.int32)
    slots = lax.broadcasted_iota(jnp.int32, (total, rows), 0)
    acc = jnp.zeros(out.shape, F32)
    for s, ref in enumerate((l0, l1, l2, l3)):
        pick = (slots == slot[:, s * rows : (s + 1) * rows]).astype(F32).astype(BF16)
        up = jnp.dot(ref[...], w[...], preferred_element_type=F32).astype(BF16)
        acc = acc + jnp.dot(pick, up, preferred_element_type=F32)
    out[...] = acc.astype(BF16)


def statistics(a_states, v_states, a_mean, a_scale, v_scale):
    inv = 1.0 / a_states.shape[1]
    h = a_states[...].astype(F32)
    mean = jnp.sum(h, axis=1, keepdims=True) * inv
    centred = h - mean
    a_mean[...] = mean
    a_scale[...] = lax.rsqrt(jnp.sum(centred * centred, axis=1, keepdims=True) * inv + 1e-5)
    g = v_states[...].astype(F32)
    v_scale[...] = lax.rsqrt(jnp.sum(g * g, axis=1, keepdims=True) * inv + 1e-6)


def upstream(recv, h, m, rows):
    column = lax.rem(m + lax.axis_index("groups"), 2)
    return recv[:, h, column].reshape(rows, recv.shape[-1]).astype(F32)


def gain_sums(recv, a_states, v_states, a_mean, a_scale, v_scale, gains):
    rows, width = a_states.shape
    half = width // 2
    sides = ((a_states, a_mean[...], a_scale), (v_states, 0.0, v_scale))
    for m, (states, mean, scale) in enumerate(sides):
        for h in range(2):
            cols = slice(h * half, (h + 1) * half)
            n = (states[:, cols].astype(F32) - mean) * scale[...]
            gains[m : m + 1, cols] = jnp.sum(upstream(recv, h, m, rows) * n, axis=0, keepdims=True)


def norms(recv, a_states, v_states, a_mean, a_scale, v_scale, a_gain, v_gain, a_out, v_out):
    rows, width = a_states.shape
    half = width // 2
    inv = 1.0 / width
    sides = ((a_states, a_mean[...], a_scale, a_gain, a_out), (v_states, 0.0, v_scale, v_gain, v_out))
    for m, (states, mean, scale, gain, out) in enumerate(sides):
        ps, pn, parts = 0.0, 0.0, []
        for h in range(2):
            cols = slice(h * half, (h + 1) * half)
            n = (states[:, cols].astype(F32) - mean) * scale[...]
            p = upstream(recv, h, m, rows) * gain[:, cols]
            ps = ps + jnp.sum(p, axis=1, keepdims=True)
            pn = pn + jnp.sum(p * n, axis=1, keepdims=True)
            parts.append((p, n, cols))
        for p, n, cols in parts:
            if m == 0:
                p = p - ps * inv
            out[:, cols] = (scale[...] * (p - n * (pn * inv))).astype(BF16)


def call(body, outs, specs, scratch=(), out_spec=VM, limit=BIG):
    return pl.pallas_call(
        body,
        out_shape=outs,
        in_specs=specs,
        out_specs=jax.tree.map(lambda _: out_spec, outs),
        scratch_shapes=list(scratch),
        compiler_params=pltpu.CompilerParams(vmem_limit_bytes=limit),
    )


def on_device(
    grad_rows,
    route_ids,
    audio_proj,
    vision_proj,
    audio_states,
    vision_states,
    audio_gain,
    vision_gain,
):
    devices = lax.axis_size("seq")
    lines = devices // 4
    rows, width = grad_rows.shape
    enc, k = audio_proj.shape
    half = enc // 2
    cap = rows // devices
    group = lax.axis_index("groups")
    me = lax.axis_index("seq")
    line, pair, core = me // 4, (me // 2) % 2, me % 2

    modality = (core + group) % 2
    ids = route_ids.reshape(1, rows)

    if lines == 4:
        block = jax.ShapeDtypeStruct((k, half), BF16)
        keep, to_pair = call(cut, (block,) * 2, [ANY, ANY], [pltpu.SemaphoreType.DMA((2,))], VM, WHOLE)(
            audio_proj.T, vision_proj.T
        )
        p = jnp.where(group == 0, line, 7 - line)
        ends, mids = (0, 3, 4, 7), (1, 2, 5, 6)
        f_own, b_own = step(keep, keep, 1, devices)
        from_pair = after(flip(to_pair, 2, devices), f_own, b_own)
        r_pair = flip(after(grad_rows, from_pair), 2, devices)
        f_far, b_far = step(from_pair, from_pair, 1, devices)
        whole = jnp.concatenate([keep, from_pair])
        f1, b1 = jnp.concatenate([f_own, f_far]), jnp.concatenate([b_own, b_far])
        r_core = flip(after(grad_rows, f1, b1), 1, devices)
        i_core = flip(after(ids, f1, b1), 1, devices)
        mirror = cycle(whole, [(a, 7 - a) for a in mids], devices)
        f2, b2 = step(f1, b1, 2, devices)
        inner = swap(f1, b1, p, mids, devices)
        f3, b3 = step(*after((f2, b2), inner, mirror), 3, devices)
        opposite = jnp.where(p % 4 < 2, b3, f3)
        over_y = cycle(opposite[:k], [(a, 7 - a) for a in ends], devices)
        along_z = cycle(opposite[k:], [(1, 0), (2, 3), (5, 4), (6, 7)], devices)
        r_there = after(r_pair, f3, b3)
        r_both = flip(r_there, 1, devices)
        late_ids = after(ids, r_there)
        i_pair, i_both = flip(late_ids, 2, devices), flip(late_ids, 3, devices)
        chain = (whole, mirror, f1, f2, f3, b1, b2, b3, inner, over_y, along_z)
        packed = call(
            product_cycle,
            jax.ShapeDtypeStruct((devices, 4, cap, half), BF16),
            [ANY] * 19,
            [
                pltpu.VMEM((4 * rows, width), BF16),
                pltpu.VMEM((width, half), BF16),
                pltpu.VMEM((4 * rows, half), F32),
                pltpu.VMEM((4, 1, rows), jnp.int32),
                pltpu.SemaphoreType.DMA((36,)),
            ],
            limit=WHOLE,
        )(ids, i_pair, i_core, i_both, *chain, grad_rows, r_pair, r_core, r_both)
    else:
        both = jnp.stack([audio_proj.T, vision_proj.T]).reshape(2, k, 2, half)
        plane = [both[modality, :, pair]]
        plane.append(flip(both[modality, :, 1 - pair], 2, devices))
        plane.append(flip(both[1 - modality, :, pair], 1, devices))
        plane.append(flip(both[1 - modality, :, 1 - pair], 3, devices))
        low = me % 4
        source = jnp.stack([low, low ^ 2, low ^ 1, low ^ 3])
        plane = jnp.zeros((4, k, half), BF16).at[source].set(jnp.stack(plane))
        ranks = [[a * 4 + w for a in range(lines)] for w in range(4)]
        w = lax.all_gather(plane.reshape(4 * k, half), "seq", axis=0, tiled=True, axis_index_groups=ranks)
        i_pair = flip(ids, 2, devices)
        i_far = flip(jnp.concatenate([ids, i_pair], axis=1), 1, devices)
        r_pair = flip(grad_rows, 2, devices)
        lhs = (grad_rows, r_pair, flip(grad_rows, 1, devices), flip(r_pair, 1, devices))
        all_ids = jnp.concatenate([ids, i_pair, i_far], axis=1)
        base = (all_ids % devices * 4 + jnp.repeat(source, rows)[None, :]) * cap
        base = jnp.where(all_ids // devices == modality, base, -(8 * rows))
        packed = call(product_plain, jax.ShapeDtypeStruct((4 * rows, half), BF16), [VM] * 7)(
            base.reshape(-1, 1), base, *lhs, w
        )

    packed = packed.reshape(devices, 4 * cap, half)
    arrived = lax.all_to_all(packed, "seq", 0, 0, tiled=True)
    arrived = arrived.reshape(lines, 2, 2, 4, cap, half)
    if cap % 16 != 0:
        arrived = arrived.transpose(1, 2, 0, 3, 4, 5).reshape(1, 2, 2, 1, rows, half)

    thin = jax.ShapeDtypeStruct((rows, 1), F32)
    states = (audio_states, vision_states)
    states += tuple(call(statistics, (thin,) * 3, [VM] * 2)(*states))
    gains = call(gain_sums, jax.ShapeDtypeStruct((2, enc), F32), [VM] * 6)(arrived, *states)
    grad = jax.ShapeDtypeStruct((rows, enc), BF16)
    audio_grad, vision_grad = call(norms, (grad, grad), [VM] * 8)(
        arrived, *states, audio_gain[None, :], vision_gain[None, :]
    )
    bit = 1
    while bit < devices:
        gains = gains + flip(gains, bit, devices)
        bit *= 2
    return (audio_grad, vision_grad, gains)


def solution(mesh):
    placed = (
        P(("groups", "seq"), None),
        P(("groups", "seq"), None),
        P(None, "seq"),
        P(None, "seq"),
        P(("groups", "seq"), None),
        P(("groups", "seq"), None),
        P(),
        P(),
    )
    return jax.shard_map(
        on_device,
        mesh=mesh,
        in_specs=placed,
        out_specs=(P(("groups", "seq"), None), P(("groups", "seq"), None), P("groups", None)),
        check_vma=False,
    )
```

```python
import functools

import jax
import jax.numpy as jnp
from jax import lax
from jax.experimental import pallas as pl
from jax.experimental.pallas import tpu as pltpu
from jax.sharding import PartitionSpec as P

F32 = jnp.float32
BF16 = jnp.bfloat16
BOTH = ("groups", "seq")
BIG = 24 * 1024 * 1024
WHOLE = 125 * 512 * 1024
VM = pl.BlockSpec(memory_space=pltpu.VMEM)
ANY = pl.BlockSpec(memory_space=pl.ANY)


def flip(value, bits, devices):
    return lax.ppermute(value, "seq", [(i, i ^ bits) for i in range(devices)])


def spot(p, low, devices):
    group, line = (0, p) if p < 4 else (1, 7 - p)
    return group * devices + line * 4 + (low ^ group)


def cycle(value, moves, devices):
    pairs = [(spot(a, w, devices), spot(b, w, devices)) for a, b in moves for w in range(4)]
    return lax.ppermute(value, BOTH, pairs)


def after(value, *others):
    return lax.optimization_barrier((value,) + others)[0]


def step(fwd, bwd, k, devices):
    up = [(a, (a + 1) % 8) for a in range(8)]
    down = [(a, (a - 1) % 8) for a in range(8)]
    if k == 3:
        up = [(a, b) for a, b in up if (b - k) % 8 != 7 - b]
        down = [(a, b) for a, b in down if (b + k) % 8 != 7 - b]
    return cycle(fwd, up, devices), cycle(bwd, down, devices)


def swap(fwd, bwd, p, spots, devices):
    first = (p % 4 == 0) | (p % 4 == 1)
    return cycle(jnp.where(first, bwd, fwd), [(a, 7 - a) for a in spots], devices)


def seat():
    me = lax.axis_index("seq")
    return lax.axis_index("groups"), me // 4, lax.rem(me // 2, 2), lax.rem(me, 2)


def cut(a_ref, v_ref, keep, to_pair, sems):
    group, _, pair, core = seat()
    half = keep.shape[1]
    near = pl.ds(pl.multiple_of(pair * half, 128), half)
    away = pl.ds(pl.multiple_of((1 - pair) * half, 128), half)
    for same in (True, False):
        mine = a_ref if same else v_ref

        @pl.when((core == group) == same)
        def _():
            pltpu.make_async_copy(mine.at[:, near], keep, sems.at[0]).start()
            pltpu.make_async_copy(mine.at[:, away], to_pair, sems.at[1]).start()

    for i, out in enumerate((keep, to_pair)):
        pltpu.make_async_copy(a_ref.at[:, near], out, sems.at[i]).wait()


def columns(line, width):
    return pl.ds(pl.multiple_of(line * (width // 4), 128), width // 4)


def line_of(q):
    return jnp.where(q < 4, q, 7 - q)


def load_rows(lhs, lines, buf, sem):
    rows, width = lhs[0].shape
    copies = []
    for j, line in enumerate(lines):
        for s, ref in enumerate(lhs):
            to = buf.at[pl.ds(s * rows, rows), pl.ds(j * (width // 4), width // 4)]
            copies.append(pltpu.make_async_copy(ref.at[:, columns(line, width)], to, sem.at[16 + j * len(lhs) + s]))
    return copies


def product_cycle(*refs):
    ids = refs[:4]
    parts, lhs = refs[4:15], refs[15:19]
    out, buf, w, acc, named, sems = refs[19:]
    deep = parts[0].shape[0] // 2
    rows = lhs[0].shape[0]
    devices, sources, cap, half = out.shape
    group, line, x, core = seat()
    modality = lax.rem(core + group, 2)
    p = jnp.where(group == 0, line, 7 - line)
    ends = lax.rem(p, 4)

    def pick(values):
        return jnp.where(ends == 0, values[0], jnp.where(ends == 1, values[1], jnp.where(ends == 2, values[2], values[3])))

    lines = [line_of(lax.rem(p + pick(far), 8)) for far in ((0, 0, 0, 0), (1, 1, 7, 7), (2, 7, 6, 6), (3, 2, 1, 5))]
    row_copies = load_rows(lhs, lines, buf, sems)

    def move(ref, far, slot, i):
        core_of = lax.rem(lax.rem(p + far, 8) // 4 + modality, 2)
        out = []
        for part in range(2):
            place = (slot * 2 + lax.rem(x + part, 2)) * 2 + core_of
            to = w.at[pl.ds(pl.multiple_of(place * deep, 16), deep)]
            src = ref[part] if isinstance(ref, tuple) else ref.at[pl.ds(part * deep, deep)]
            out.append(pltpu.make_async_copy(src, to, sems.at[4 * slot + 2 * i + part]))
        return out

    def start(slot):
        for c in row_copies[4 * slot : 4 * slot + 4]:
            c.start()
        own, mirror, f1, f2, f3, b1, b2, b3, inner = parts[:9]
        outer = (parts[9], parts[10])
        turn = 7 + 6 * p
        behind, ahead = (f1, turn), (b1, turn)
        f1, f2, f3, b1, b2, b3 = (f1, 7), (f2, 6), (f3, 5), (b1, 1), (b2, 2), (b3, 3)
        inner, outer, own, mirror = (inner, 4), (outer, 4), (own, 0), (mirror, turn)
        takes = (
            ((own, behind), (own, mirror), (own, mirror), (own, ahead)),
            ((b1, f2), (b1, inner), (f1, inner), (f1, b2)),
            ((b2, f3), (f1, f2), (f2, f3), (f2, b3)),
            ((b3, outer), (b2, b3), (b1, b2), (f3, outer)),
        )[slot]
        for case in range(4):

            @pl.when(ends == case)
            def _():
                for i, (ref, far) in enumerate(takes[case]):
                    for c in move(ref, far, slot, i):
                        c.start()

    def wait(slot):
        for c in row_copies[4 * slot : 4 * slot + 4]:
            c.wait()
        for i in range(2):
            for c in move(parts[0], 0, slot, i):
                c.wait()

    id_copies = [pltpu.make_async_copy(ref, named.at[s], sems.at[32 + s]) for s, ref in enumerate(ids)]
    for c in id_copies:
        c.start()
    start(0)
    start(1)
    earlier = lax.broadcasted_iota(jnp.int32, (rows, rows), 0) < lax.broadcasted_iota(jnp.int32, (rows, rows), 1)
    earlier = earlier.astype(F32).astype(BF16)
    kinds = lax.broadcasted_iota(jnp.int32, (devices, rows), 0) + modality * devices
    slots = lax.broadcasted_iota(jnp.int32, (devices * cap, rows), 0)
    picks = []
    for c in id_copies:
        c.wait()
    for s in range(4):
        named_by = named[s]
        hit = (kinds == named_by).astype(F32)
        before = jnp.dot(hit.astype(BF16), earlier, preferred_element_type=F32)
        count = jnp.sum(hit * before, axis=0, keepdims=True).astype(jnp.int32)
        slot = (named_by - modality * devices) * cap + count
        picks.append((slots == slot).astype(F32).astype(BF16))
    low = x * 2 + core
    source = (low, (1 - x) * 2 + core, x * 2 + 1 - core, (1 - x) * 2 + 1 - core)
    wait(0)
    wait(1)
    start(2)
    start(3)
    span = slice(0, 8 * deep)
    acc[...] = jnp.dot(buf[:, span], w[span, :], preferred_element_type=F32)
    wait(2)
    wait(3)
    span = slice(8 * deep, 16 * deep)
    for s in range(4):
        at = slice(s * rows, (s + 1) * rows)
        up = acc[at, :] + jnp.dot(buf[at, span], w[span, :], preferred_element_type=F32)
        packed = jnp.dot(picks[s], up.astype(BF16), preferred_element_type=F32).astype(BF16)
        out[:, source[s]] = packed.reshape(devices, cap, half)


def product_plain(base_col, base_row, l0, l1, l2, l3, w, out):
    rows = l0.shape[0]
    total = 4 * rows
    first = lax.broadcasted_iota(jnp.int32, (total, total), 0)
    second = lax.broadcasted_iota(jnp.int32, (total, total), 1)
    same = jnp.logical_and(base_col[...] == base_row[...], first < second)
    slot = base_row[...] + jnp.sum(same.astype(F32), axis=0, keepdims=True).astype(jnp.int32)
    slots = lax.broadcasted_iota(jnp.int32, (total, rows), 0)
    acc = jnp.zeros(out.shape, F32)
    for s, ref in enumerate((l0, l1, l2, l3)):
        pick = (slots == slot[:, s * rows : (s + 1) * rows]).astype(F32).astype(BF16)
        up = jnp.dot(ref[...], w[...], preferred_element_type=F32).astype(BF16)
        acc = acc + jnp.dot(pick, up, preferred_element_type=F32)
    out[...] = acc.astype(BF16)


def statistics(a_states, v_states, a_mean, a_scale, v_scale):
    inv = 1.0 / a_states.shape[1]
    h = a_states[...].astype(F32)
    mean = jnp.sum(h, axis=1, keepdims=True) * inv
    centred = h - mean
    a_mean[...] = mean
    a_scale[...] = lax.rsqrt(jnp.sum(centred * centred, axis=1, keepdims=True) * inv + 1e-5)
    g = v_states[...].astype(F32)
    v_scale[...] = lax.rsqrt(jnp.sum(g * g, axis=1, keepdims=True) * inv + 1e-6)


def upstream(recv, h, m, rows):
    column = lax.rem(m + lax.axis_index("groups"), 2)
    return recv[:, h, column].reshape(rows, recv.shape[-1]).astype(F32)


def gain_sums(recv, a_states, v_states, a_mean, a_scale, v_scale, gains):
    rows, width = a_states.shape
    half = width // 2
    sides = ((a_states, a_mean[...], a_scale), (v_states, 0.0, v_scale))
    for m, (states, mean, scale) in enumerate(sides):
        for h in range(2):
            cols = slice(h * half, (h + 1) * half)
            n = (states[:, cols].astype(F32) - mean) * scale[...]
            gains[m : m + 1, cols] = jnp.sum(upstream(recv, h, m, rows) * n, axis=0, keepdims=True)


def norms(recv, a_states, v_states, a_mean, a_scale, v_scale, a_gain, v_gain, a_out, v_out):
    rows, width = a_states.shape
    half = width // 2
    inv = 1.0 / width
    sides = ((a_states, a_mean[...], a_scale, a_gain, a_out), (v_states, 0.0, v_scale, v_gain, v_out))
    for m, (states, mean, scale, gain, out) in enumerate(sides):
        ps, pn, parts = 0.0, 0.0, []
        for h in range(2):
            cols = slice(h * half, (h + 1) * half)
            n = (states[:, cols].astype(F32) - mean) * scale[...]
            p = upstream(recv, h, m, rows) * gain[:, cols]
            ps = ps + jnp.sum(p, axis=1, keepdims=True)
            pn = pn + jnp.sum(p * n, axis=1, keepdims=True)
            parts.append((p, n, cols))
        for p, n, cols in parts:
            if m == 0:
                p = p - ps * inv
            out[:, cols] = (scale[...] * (p - n * (pn * inv))).astype(BF16)


def call(body, outs, specs, scratch=(), out_spec=VM, limit=BIG):
    return pl.pallas_call(
        body,
        out_shape=outs,
        in_specs=specs,
        out_specs=jax.tree.map(lambda _: out_spec, outs),
        scratch_shapes=list(scratch),
        compiler_params=pltpu.CompilerParams(vmem_limit_bytes=limit),
    )


def on_device(
    grad_rows,
    route_ids,
    audio_proj,
    vision_proj,
    audio_states,
    vision_states,
    audio_gain,
    vision_gain,
):
    devices = lax.axis_size("seq")
    lines = devices // 4
    rows, width = grad_rows.shape
    enc, k = audio_proj.shape
    half = enc // 2
    cap = rows // devices
    group = lax.axis_index("groups")
    me = lax.axis_index("seq")
    line, pair, core = me // 4, (me // 2) % 2, me % 2

    modality = (core + group) % 2
    ids = route_ids.reshape(1, rows)

    if lines == 4:
        block = jax.ShapeDtypeStruct((k, half), BF16)
        keep, to_pair = call(cut, (block,) * 2, [ANY, ANY], [pltpu.SemaphoreType.DMA((2,))], VM, WHOLE)(
            audio_proj.T, vision_proj.T
        )
        p = jnp.where(group == 0, line, 7 - line)
        ends, mids = (0, 3, 4, 7), (1, 2, 5, 6)
        f_own, b_own = step(keep, keep, 1, devices)
        i_core, i_pair, i_both = (flip(after(ids, to_pair), bits, devices) for bits in (1, 2, 3))
        from_pair = after(flip(to_pair, 2, devices), f_own, b_own)
        r_pair = flip(after(grad_rows, from_pair, i_core, i_pair, i_both), 2, devices)
        f_far, b_far = step(from_pair, from_pair, 1, devices)
        whole = jnp.concatenate([keep, from_pair])
        f1, b1 = jnp.concatenate([f_own, f_far]), jnp.concatenate([b_own, b_far])
        r_core = flip(after(grad_rows, f1, b1), 1, devices)
        mirror = cycle(whole, [(a, 7 - a) for a in mids], devices)
        f2, b2 = step(f1, b1, 2, devices)
        inner = swap(f1, b1, p, mids, devices)
        f3, b3 = step(*after((f2, b2), inner, mirror), 3, devices)
        opposite = jnp.where(p % 4 < 2, b3, f3)
        over_y = cycle(opposite[:k], [(a, 7 - a) for a in ends], devices)
        along_z = cycle(opposite[k:], [(1, 0), (2, 3), (5, 4), (6, 7)], devices)
        r_both = flip(after(r_pair, f3, b3), 1, devices)
        chain = (whole, mirror, f1, f2, f3, b1, b2, b3, inner, over_y, along_z)
        packed = call(
            product_cycle,
            jax.ShapeDtypeStruct((devices, 4, cap, half), BF16),
            [ANY] * 19,
            [
                pltpu.VMEM((4 * rows, width), BF16),
                pltpu.VMEM((width, half), BF16),
                pltpu.VMEM((4 * rows, half), F32),
                pltpu.VMEM((4, 1, rows), jnp.int32),
                pltpu.SemaphoreType.DMA((36,)),
            ],
            limit=WHOLE,
        )(ids, i_pair, i_core, i_both, *chain, grad_rows, r_pair, r_core, r_both)
    else:
        both = jnp.stack([audio_proj.T, vision_proj.T]).reshape(2, k, 2, half)
        plane = [both[modality, :, pair]]
        plane.append(flip(both[modality, :, 1 - pair], 2, devices))
        plane.append(flip(both[1 - modality, :, pair], 1, devices))
        plane.append(flip(both[1 - modality, :, 1 - pair], 3, devices))
        low = me % 4
        source = jnp.stack([low, low ^ 2, low ^ 1, low ^ 3])
        plane = jnp.zeros((4, k, half), BF16).at[source].set(jnp.stack(plane))
        ranks = [[a * 4 + w for a in range(lines)] for w in range(4)]
        w = lax.all_gather(plane.reshape(4 * k, half), "seq", axis=0, tiled=True, axis_index_groups=ranks)
        i_pair = flip(ids, 2, devices)
        i_far = flip(jnp.concatenate([ids, i_pair], axis=1), 1, devices)
        r_pair = flip(grad_rows, 2, devices)
        lhs = (grad_rows, r_pair, flip(grad_rows, 1, devices), flip(r_pair, 1, devices))
        all_ids = jnp.concatenate([ids, i_pair, i_far], axis=1)
        base = (all_ids % devices * 4 + jnp.repeat(source, rows)[None, :]) * cap
        base = jnp.where(all_ids // devices == modality, base, -(8 * rows))
        packed = call(product_plain, jax.ShapeDtypeStruct((4 * rows, half), BF16), [VM] * 7)(
            base.reshape(-1, 1), base, *lhs, w
        )

    packed = packed.reshape(devices, 4 * cap, half)
    arrived = lax.all_to_all(packed, "seq", 0, 0, tiled=True)
    arrived = arrived.reshape(lines, 2, 2, 4, cap, half)
    if cap % 16 != 0:
        arrived = arrived.transpose(1, 2, 0, 3, 4, 5).reshape(1, 2, 2, 1, rows, half)

    thin = jax.ShapeDtypeStruct((rows, 1), F32)
    states = (audio_states, vision_states)
    states += tuple(call(statistics, (thin,) * 3, [VM] * 2)(*states))
    gains = call(gain_sums, jax.ShapeDtypeStruct((2, enc), F32), [VM] * 6)(arrived, *states)
    grad = jax.ShapeDtypeStruct((rows, enc), BF16)
    audio_grad, vision_grad = call(norms, (grad, grad), [VM] * 8)(
        arrived, *states, audio_gain[None, :], vision_gain[None, :]
    )
    bit = 1
    while bit < devices:
        gains = gains + flip(gains, bit, devices)
        bit *= 2
    return (audio_grad, vision_grad, gains)


def solution(mesh):
    placed = (
        P(("groups", "seq"), None),
        P(("groups", "seq"), None),
        P(None, "seq"),
        P(None, "seq"),
        P(("groups", "seq"), None),
        P(("groups", "seq"), None),
        P(),
        P(),
    )
    return jax.shard_map(
        on_device,
        mesh=mesh,
        in_specs=placed,
        out_specs=(P(("groups", "seq"), None), P(("groups", "seq"), None), P("groups", None)),
        check_vma=False,
    )
```
